512 devices in a mesh: dp: 32 (over x, y), bucket: 16 (over z, core).
Axes of the slice: x: 4, y: 8, z: 8, core: 2. Of those that a mesh axis runs over, the one named last changes fastest.
Arguments:
- embeddings: float32 [65536, 256], P('dp'), may hold values from -40 to 40, as said below
- prototypes: float32 [16384, 256], P('bucket'), may hold values from -6 to 6, as said below
Outputs:
- new_protos: float32 [16384, 256], P('bucket')
- col_pot: float32 [16384], P('bucket')
The draws below stay inside these ranges and needn't reach their ends.
Inputs may be any that keep to these rules, and one draw needn't show every extreme that they name: Real-valued embeddings. Real-valued prototypes.
All inputs are finite; a program needn't handle non-finite values.
Results may differ from the reference program's by a relative error of at most 0.0003.
Values sent between devices are 32-bit elements; how exact they have to be, the bound alone decides.
A program may use at most 64 MiB of HBM per device.

```python
import math
import jax
import jax.numpy as jnp
from jax import lax

DW = 256
ROWS_DEV = 2048
ITERS = 3
K = 16384
EMBEDDING_ROWS = 65536
N_DP = 32


def base_protos(key):
    first = jax.random.fold_in(jax.random.fold_in(key, 101), 0)
    table = jnp.clip(jax.random.normal(first, (K, DW), jnp.float32), -5.0, 5.0)
    return table


def draw_prototypes(key, part):
    return base_protos(key)


def draw_embeddings(key, part):
    key_norm_value, key_scale_factor = jax.random.split(jax.random.fold_in(key, 202), 2)
    value_entries = jnp.clip(jax.random.normal(key_norm_value, (EMBEDDING_ROWS, DW), jnp.float32), -4.0, 4.0)
    value_entries = value_entries * jnp.exp(jax.random.uniform(key_scale_factor, (EMBEDDING_ROWS, 1), jnp.float32) * math.log(10.0))
    return jnp.clip(value_entries, -40.0, 40.0)


def setup_inputs(seed: int = 0) -> dict:
    seeds = jax.random.split(jax.random.key(seed), 3)
    return {
        "embeddings": draw_embeddings(jax.random.fold_in(seeds[2], 71), 0),
        "prototypes": draw_prototypes(jax.random.fold_in(seeds[2], 71), 0),
    }


def reference(embeddings, prototypes):
    sharp = 2.0 / math.sqrt(DW)
    blocks = embeddings.reshape(N_DP, ROWS_DEV, DW)
    log_rows = math.log(EMBEDDING_ROWS)
    log_cols = math.log(K)

    def logits_of(block):
        return jnp.dot(block, prototypes.T, precision=lax.Precision.HIGHEST, preferred_element_type=jnp.float32) * sharp
    col_pot = jnp.zeros((K,), jnp.float32)
    row_pots = None
    for step in range(ITERS):

        def sweep(carry, block, col_pot=col_pot):
            peak, mass = carry
            logits = logits_of(block)
            row_pot = -log_rows - jax.nn.logsumexp(logits + col_pot[None, :], axis=1)
            shifted = logits + row_pot[:, None]
            new_peak = jnp.maximum(peak, lax.optimization_barrier(jnp.max(shifted, axis=0)))
            mass = mass * jnp.exp(peak - new_peak) + lax.optimization_barrier(jnp.sum(jnp.exp(shifted - new_peak[None, :]), axis=0))
            return ((new_peak, mass), row_pot)
        start = (jnp.full((K,), -jnp.inf, jnp.float32), jnp.zeros((K,), jnp.float32))
        (peak, mass), row_pots = lax.scan(sweep, start, blocks)
        col_pot = -log_cols - (peak + jnp.log(mass))

    def accumulate(total, item):
        block, row_pot = item
        weights = jnp.exp(logits_of(block) + row_pot[:, None] + col_pot[None, :])
        return (total + jnp.dot(weights.T, block, precision=lax.Precision.HIGHEST, preferred_element_type=jnp.float32), None)
    centers, unused = lax.scan(accumulate, jnp.zeros((K, DW), jnp.float32), (blocks, row_pots))
    centers = centers * float(K)
    new_protos = centers * lax.rsqrt(lax.optimization_barrier(jnp.mean(centers * centers, axis=1, keepdims=True)) + 1e-06)
    return (new_protos, col_pot)
```

```python
import functools
import math

import jax
import jax.numpy as jnp
from jax import lax
from jax.experimental import pallas as pl
from jax.experimental.pallas import tpu as pltpu
from jax.sharding import PartitionSpec as P

NX, NY, NZ, NC = 4, 8, 8, 2
NDP = NX * NY
MESH = pl.DeviceIdType.MESH
F32 = jnp.float32
BF16 = jnp.bfloat16
LN2 = math.log(2.0)

ROWS = 2048
PROT = 1024
DW = 256
TOTAL_ROWS = ROWS * NDP
TOTAL_PROT = PROT * NZ * NC

XROWS = 768
XC1, XC2 = XROWS // NX, XROWS // NDP
YROWS = PROT - XROWS
YC1, YC2 = YROWS // NY, YROWS // NDP


def split(x):
    hi = x.astype(BF16)
    return hi, (x - hi.astype(F32)).astype(BF16)


def nt(a, b):
    return lax.dot_general(a, b, (((1,), (1,)), ((), ())), preferred_element_type=F32)


def nn(a, b):
    return lax.dot_general(a, b, (((1,), (0,)), ((), ())), preferred_element_type=F32)


def lanes(x, reduce):
    parts = [x[:, 128 * t : 128 * (t + 1)] for t in range(x.shape[1] // 128)]
    while len(parts) > 1:
        parts = [reduce(a, b) for a, b in zip(parts[::2], parts[1::2])]
    return parts[0]


def log_sum(terms):
    peak = functools.reduce(jnp.maximum, terms)
    mass = functools.reduce(jnp.add, [jnp.exp2(t - peak) for t in terms])
    return peak + jnp.log2(mass)


def total(terms):
    return functools.reduce(jnp.add, terms)


def kernel(
    e_hbm, p_hbm, cent_hbm, pot_ref,
    e_ref, p_ref, p3_ref, mat, hi_ref, lo_ref, sc_ref, part, wide, peaks, ewide, eh2, el2, lam,
    pair_buf, z_buf, xy_buf, vec_row, vec_col, sums, xb1, xb2, yb1, yb2, out,
    load_sem, ps, pr, zs, zr, cs, cr, fs, fr,
):
    dp, bk = lax.axis_index("dp"), lax.axis_index("bucket")
    x, y = dp // NY, dp % NY
    z, c = bk // NC, bk % NC

    load_p = pltpu.make_async_copy(p_hbm, p_ref, load_sem.at[0])
    load_e = pltpu.make_async_copy(e_hbm, e_ref, load_sem.at[1])
    load_p.start()
    load_e.start()

    pair_dev = (dp, z * NC + (1 - c))

    def z_dev(d):
        return (dp, ((z + d) % NZ) * NC + c)

    def xy_dev(dx, dy):
        return (((x + dx) % NX) * NY + (y + dy) % NY, bk)

    xy_peers = sorted(
        [(dx, dy) for dx in range(NX) for dy in range(NY) if dx or dy],
        key=lambda p: -(min(p[0], NX - p[0]) + min(p[1], NY - p[1])),
    )
    z_peers = sorted(range(1, NZ), key=lambda d: -min(d, NZ - d))
    x_peers, y_peers = [2, 1, 3], [4, 3, 5, 2, 6, 1, 7]

    barrier = pltpu.get_barrier_semaphore()
    everyone = [pair_dev] + [z_dev(d) for d in z_peers] + [xy_dev(*p) for p in xy_peers]
    for d in everyone:
        pl.semaphore_signal(barrier, 1, device_id=d, device_id_type=MESH)

    load_p.wait()
    ph, plo = split(p_ref[...] * F32(2.0 / math.sqrt(DW) / LN2))
    p3_ref[:, 0:DW] = ph
    p3_ref[:, DW : 2 * DW] = ph
    p3_ref[:, 2 * DW :] = plo
    load_e.wait()

    CH = 256

    def logits_chunk(j, _):
        r0 = pl.multiple_of(j * CH, CH)
        eh, el = split(e_ref[pl.ds(r0, CH), :])
        e3 = jnp.concatenate([eh, el, eh], axis=1)
        mat[:, pl.ds(r0, CH)] = nt(p3_ref[...], e3)

        def peak_step(g, m):
            return jnp.maximum(m, mat[pl.ds(pl.multiple_of(g * 8, 8), 8), pl.ds(r0, CH)])

        m = lax.fori_loop(0, PROT // 8, peak_step, jnp.full((8, CH), -jnp.inf, F32), unroll=16)
        m = jnp.max(m, axis=0, keepdims=True)

        def mass_step(g, s):
            return s + jnp.exp2(mat[pl.ds(pl.multiple_of(g * 8, 8), 8), pl.ds(r0, CH)] - m)

        s = lax.fori_loop(0, PROT // 8, mass_step, jnp.zeros((8, CH), F32), unroll=16)
        lam[:, pl.ds(r0, CH)] = m + jnp.log2(jnp.sum(s, axis=0, keepdims=True))
        return 0

    lax.fori_loop(0, ROWS // CH, logits_chunk, 0)

    pl.semaphore_wait(barrier, len(everyone))

    def row_exchange(n, vec, combine):
        vec_row[n] = vec
        cp = pltpu.make_async_remote_copy(
            vec_row.at[n], pair_buf.at[n], ps.at[n], pr.at[n], device_id=pair_dev, device_id_type=MESH)
        cp.start()
        cp.wait()
        mine = combine([vec, pair_buf[n]])
        z_buf[n, z] = mine
        for d in z_peers:
            pltpu.make_async_remote_copy(
                z_buf.at[n, z], z_buf.at[n, z], zs.at[n], zr.at[n], device_id=z_dev(d), device_id_type=MESH).start()
        seven = z_buf.at[n, pl.ds(0, NZ - 1)]
        pltpu.make_async_copy(seven, seven, zr.at[n]).wait()
        pltpu.make_async_copy(seven, seven, zs.at[n]).wait()
        return combine([z_buf[n, d] for d in range(NZ)])

    def col_send(n, vec):
        xy_buf[n, dp] = vec
        for p in xy_peers:
            pltpu.make_async_remote_copy(
                xy_buf.at[n, dp], xy_buf.at[n, dp], cs.at[n], cr.at[n], device_id=xy_dev(*p), device_id_type=MESH).start()

    def col_wait(n, combine):
        rest = xy_buf.at[n, pl.ds(0, NDP - 1)]
        pltpu.make_async_copy(rest, rest, cr.at[n]).wait()
        pltpu.make_async_copy(rest, rest, cs.at[n]).wait()
        return combine([xy_buf[n, d] for d in range(NDP)])

    def to_lanes(src, reduce):
        return jnp.concatenate(
            [reduce(src[128 * a : 128 * (a + 1), :].T, axis=0, keepdims=True) for a in range(PROT // 128)], axis=0)

    def to_wide(dst, vec, n):
        for a in range(n):
            dst[128 * a : 128 * (a + 1), :] = jnp.broadcast_to(vec[a : a + 1, :], (128, 128)).T

    def group(g):
        return pl.ds(pl.multiple_of(g * 8, 8), 8)

    def row_sums():
        def step(g, acc):
            v = wide[group(g), :]
            return acc + mat[group(g), :] * jnp.concatenate([v] * (ROWS // 128), axis=1)

        acc = lax.fori_loop(0, PROT // 8, step, jnp.zeros((8, ROWS), F32), unroll=4)
        return jnp.sum(acc, axis=0, keepdims=True)

    def col_sums(u):
        ub = jnp.broadcast_to(u, (8, ROWS))

        def step(g, _):
            part[group(g), :] = lanes(mat[group(g), :] * ub, jnp.add)
            return 0

        lax.fori_loop(0, PROT // 8, step, 0, unroll=4)
        return to_lanes(part, jnp.sum)

    r_log = row_exchange(0, lam[...], log_sum)

    rb = jnp.broadcast_to(r_log, (8, ROWS))

    def peak_group(g, _):
        part[group(g), :] = lanes(mat[group(g), :] - rb, jnp.maximum)
        return 0

    lax.fori_loop(0, PROT // 8, peak_group, 0, unroll=4)
    peak = to_lanes(part, jnp.max)
    to_wide(peaks, peak, PROT // 128)

    def exp_group(g, _):
        m = peaks[group(g), :]
        b = jnp.exp2(mat[group(g), :] - rb - jnp.concatenate([m] * (ROWS // 128), axis=1))
        mat[group(g), :] = b
        part[group(g), :] = lanes(b, jnp.add)
        return 0

    lax.fori_loop(0, PROT // 8, exp_group, 0, unroll=2)
    col_send(0, peak + jnp.log2(to_lanes(part, jnp.sum)))

    def halves(g, _):
        rows = pl.ds(pl.multiple_of(g * 16, 16), 16)
        h, l = split(mat[rows, :])
        hi_ref[rows, :] = h
        lo_ref[rows, :] = l
        return 0

    lax.fori_loop(0, PROT // 16, halves, 0, unroll=2)

    g_log = col_wait(0, log_sum)
    w = jnp.exp2(peak - g_log)
    ratio = TOTAL_ROWS / TOTAL_PROT
    to_wide(wide, w * ratio, PROT // 128)
    u = 1.0 / row_exchange(1, row_sums(), total)
    col_send(1, w * col_sums(u))
    mass = col_wait(1, total)
    to_wide(wide, w * ratio / mass, PROT // 128)
    u = 1.0 / row_exchange(2, row_sums(), total)

    vec_row[3] = u
    for a in range(ROWS // 128):
        ewide[128 * a : 128 * (a + 1), :] = jnp.broadcast_to(u[:, 128 * a : 128 * (a + 1)], (128, 128)).T
    to_wide(wide, w, PROT // 128)

    def scale_rows(g, _):
        rows = pl.ds(pl.multiple_of(g * 16, 16), 16)
        uw = ewide[rows, :]
        h, l = split(e_ref[rows, :] * jnp.concatenate([uw, uw], axis=1))
        eh2[rows, :] = h
        el2[rows, :] = l
        return 0

    lax.fori_loop(0, ROWS // 16, scale_rows, 0, unroll=4)

    def product(j, _):
        rows = pl.ds(pl.multiple_of(j * 256, 256), 256)
        h = hi_ref[rows, :]
        acc = nn(h, eh2[...]) + nn(h, el2[...]) + nn(lo_ref[rows, :], eh2[...])
        ww = wide[rows, :]
        sums[rows, :] = acc * jnp.concatenate([ww, ww], axis=1)
        return 0

    lax.fori_loop(0, PROT // 256, product, 0)

    def rows_of(base, unit, index):
        return pl.ds(pl.multiple_of(base + unit * index, 8), unit)

    def send(src, dst, n, device):
        pltpu.make_async_remote_copy(src, dst, fs.at[n], fr.at[n], device_id=device, device_id_type=MESH).start()

    def await_bytes(ref, sem):
        pltpu.make_async_copy(ref, ref, sem).wait()

    for d in x_peers:
        send(sums.at[rows_of(0, XC1, (x + d) % NX)], xb1.at[x], 0, xy_dev(d, 0))
    for d in y_peers:
        send(sums.at[rows_of(XROWS, YC1, (y + d) % NY)], yb1.at[y], 1, xy_dev(0, d))

    col_send(2, w * col_sums(u))

    xb1[x] = sums[rows_of(0, XC1, x), :]
    yb1[y] = sums[rows_of(XROWS, YC1, y), :]
    await_bytes(xb1.at[pl.ds(0, NX - 1)], fr.at[0])
    sc_ref[0:XC1, :] = total([xb1[d] for d in range(NX)])
    for d in y_peers:
        send(sc_ref.at[rows_of(0, XC2, (y + d) % NY)], xb2.at[y], 2, xy_dev(0, d))
    await_bytes(yb1.at[pl.ds(0, NY - 1)], fr.at[1])
    sc_ref[XC1 : XC1 + YC1, :] = total([yb1[d] for d in range(NY)])
    for d in x_peers:
        send(sc_ref.at[rows_of(XC1, YC2, (x + d) % NX)], yb2.at[x], 3, xy_dev(d, 0))

    mass = col_wait(2, total)
    pot_ref[...] = (math.log(TOTAL_ROWS / TOTAL_PROT) - LN2 * g_log) - jnp.log(mass)
    to_wide(part, 1.0 / mass, PROT // 128)

    def finish(terms, rows):
        s = part[rows, :]
        v = total(terms) * jnp.concatenate([s, s], axis=1)
        return v * lax.rsqrt(jnp.mean(v * v, axis=1, keepdims=True) + 1e-06)

    xb2[y] = sc_ref[rows_of(0, XC2, y), :]
    yb2[x] = sc_ref[rows_of(XC1, YC2, x), :]
    await_bytes(xb2.at[pl.ds(0, NY - 1)], fr.at[2])
    x_own = rows_of(0, XC2, x * NY + y)
    out[x_own, :] = finish([xb2[d] for d in range(NY)], x_own)
    for d in y_peers:
        send(out.at[x_own], out.at[x_own], 4, xy_dev(0, d))
    await_bytes(yb2.at[pl.ds(0, NX - 1)], fr.at[3])
    y_own = rows_of(XROWS, YC2, y * NX + x)
    out[y_own, :] = finish([yb2[d] for d in range(NX)], y_own)
    for d in x_peers:
        send(out.at[y_own], out.at[y_own], 5, xy_dev(d, 0))

    await_bytes(out.at[pl.ds(0, XC1 - XC2)], fr.at[4])
    x_mid = rows_of(0, XC1, x)
    for d in x_peers:
        send(out.at[x_mid], out.at[x_mid], 6, xy_dev(d, 0))
    await_bytes(out.at[pl.ds(0, YC1 - YC2)], fr.at[5])
    y_mid = rows_of(XROWS, YC1, y)
    for d in y_peers:
        send(out.at[y_mid], out.at[y_mid], 7, xy_dev(0, d))
    await_bytes(out.at[pl.ds(0, XROWS - XC1)], fr.at[6])
    await_bytes(out.at[pl.ds(0, YROWS - YC1)], fr.at[7])
    store = pltpu.make_async_copy(out, cent_hbm, load_sem.at[0])
    store.start()
    for n, size in enumerate((XROWS - XC1, YROWS - YC1, XC1 - XC2, YC1 - YC2, XC1 - XC2, YC1 - YC2, XROWS - XC1, YROWS - YC1)):
        await_bytes(out.at[pl.ds(0, size)], fs.at[n])
    store.wait()


def body(embeddings, prototypes):
    vm = pltpu.VMEM
    dma = pltpu.SemaphoreType.DMA
    new_protos, pot = pl.pallas_call(
        kernel,
        out_shape=(
            jax.ShapeDtypeStruct((PROT, DW), F32),
            jax.ShapeDtypeStruct((8, 128), F32),
        ),
        in_specs=[pl.BlockSpec(memory_space=pl.ANY)] * 2,
        out_specs=(pl.BlockSpec(memory_space=pl.ANY), pl.BlockSpec(memory_space=vm)),
        scratch_shapes=[
            vm((ROWS, DW), F32),
            vm((PROT, DW), F32),
            vm((PROT, 3 * DW), BF16),
            vm((PROT, ROWS), F32),
            vm((PROT, ROWS), BF16),
            vm((PROT, ROWS), BF16),
            vm((XC1 + YC1, DW), F32),
            vm((PROT, 128), F32),
            vm((PROT, 128), F32),
            vm((PROT, 128), F32),
            vm((ROWS, 128), F32),
            vm((ROWS, DW), BF16),
            vm((ROWS, DW), BF16),
            vm((1, ROWS), F32),
            vm((3, 1, ROWS), F32),
            vm((3, NZ, 1, ROWS), F32),
            vm((3, NDP, 8, 128), F32),
            vm((4, 1, ROWS), F32),
            vm((3, 8, 128), F32),
            vm((PROT, DW), F32),
            vm((NX, XC1, DW), F32),
            vm((NY, XC2, DW), F32),
            vm((NY, YC1, DW), F32),
            vm((NX, YC2, DW), F32),
            vm((PROT, DW), F32),
            dma((2,)),
            dma((3,)), dma((3,)),
            dma((3,)), dma((3,)),
            dma((3,)), dma((3,)),
            dma((8,)), dma((8,)),
        ],
        compiler_params=pltpu.CompilerParams(
            collective_id=0, has_side_effects=True, vmem_limit_bytes=56 * 1024 * 1024),
        name="sinkhorn",
    )(embeddings, prototypes)
    return new_protos, pot.reshape(PROT)


def solution(mesh):
    in_specs = (P("dp", None), P("bucket", None))
    out_specs = (P("bucket", None), P("bucket"))
    return jax.shard_map(body, mesh=mesh, in_specs=in_specs, out_specs=out_specs, check_vma=False)
```

```python
import functools
import math

import jax
import jax.numpy as jnp
from jax import lax
from jax.experimental import pallas as pl
from jax.experimental.pallas import tpu as pltpu
from jax.sharding import PartitionSpec as P

NX, NY, NZ, NC = 4, 8, 8, 2
NDP = NX * NY
MESH = pl.DeviceIdType.MESH
F32 = jnp.float32
BF16 = jnp.bfloat16
LN2 = math.log(2.0)

ROWS = 2048
PROT = 1024
DW = 256
TOTAL_ROWS = ROWS * NDP
TOTAL_PROT = PROT * NZ * NC

CH = 256
NCH = ROWS // CH
BLK = 64
PARTS = ((0, 256, "y"), (256, 256, "x"), (512, 256, "x"), (768, 256, "x"))


def split(x):
    hi = x.astype(BF16)
    return hi, (x - hi.astype(F32)).astype(BF16)


def nt(a, b):
    return lax.dot_general(a, b, (((1,), (1,)), ((), ())), preferred_element_type=F32)


def nn(a, b):
    return lax.dot_general(a, b, (((1,), (0,)), ((), ())), preferred_element_type=F32)


def tree(parts, op):
    while len(parts) > 1:
        parts = [op(a, b) for a, b in zip(parts[::2], parts[1::2])]
    return parts[0]


def twice(v):
    return jnp.concatenate([v, v], axis=1)


def fold(v, op):
    return op(v[:, :128], v[:, 128:])


def log_sum(terms):
    peak = functools.reduce(jnp.maximum, terms)
    mass = functools.reduce(jnp.add, [jnp.exp2(t - peak) for t in terms])
    return peak + jnp.log2(mass)


def total(terms):
    return functools.reduce(jnp.add, terms)


def kernel(*refs):
    (e_hbm, p_hbm, out, pot_ref, e_ref, p_ref, p3_ref), refs = refs[:7], refs[7:]
    mats, refs = refs[:NCH], refs[NCH:]
    b1s, refs = refs[: len(PARTS)], refs[len(PARTS) :]
    mids, refs = refs[: len(PARTS)], refs[len(PARTS) :]
    b2s, refs = refs[: len(PARTS)], refs[len(PARTS) :]
    (hi_ref, lo_ref, part, wide, peaks, ewide, eh2, el2, lam, rb_ref, pair_buf, z_buf, xy_buf, vec_row, sums,
     load_sem, ps, pr, zs, zr, cs, cr, fs, fr) = refs
    dp, bk = lax.axis_index("dp"), lax.axis_index("bucket")
    x, y = dp // NY, dp % NY
    z, c = bk // NC, bk % NC

    load_p = pltpu.make_async_copy(p_hbm, p_ref, load_sem.at[NCH])
    load_p.start()
    loads = []
    for j in range(NCH):
        rows = pl.ds(CH * j, CH)
        loads.append(pltpu.make_async_copy(e_hbm.at[rows], e_ref.at[rows], load_sem.at[j]))
        loads[-1].start()

    pair_dev = (dp, z * NC + (1 - c))

    def z_dev(d):
        return (dp, ((z + d) % NZ) * NC + c)

    def xy_dev(dx, dy):
        return (((x + dx) % NX) * NY + (y + dy) % NY, bk)

    xy_peers = sorted(
        [(dx, dy) for dx in range(NX) for dy in range(NY) if dx or dy],
        key=lambda p: -(min(p[0], NX - p[0]) + min(p[1], NY - p[1])),
    )
    z_peers = sorted(range(1, NZ), key=lambda d: -min(d, NZ - d))
    x_peers, y_peers = [2, 1, 3], [4, 3, 5, 2, 6, 1, 7]

    barrier = pltpu.get_barrier_semaphore()
    everyone = [pair_dev] + [z_dev(d) for d in z_peers] + [xy_dev(*p) for p in xy_peers]
    for d in everyone:
        pl.semaphore_signal(barrier, 1, device_id=d, device_id_type=MESH)

    load_p.wait()
    ph, plo = split(p_ref[...] * F32(2.0 / math.sqrt(DW) / LN2))
    p3_ref[:, 0:DW] = ph
    p3_ref[:, DW : 2 * DW] = ph
    p3_ref[:, 2 * DW :] = plo

    def deep(v, op):
        v = op(op(v.reshape(PROT // 32, 4, 8, CH), axis=0), axis=0)
        return op(v, axis=0, keepdims=True)

    for j in range(NCH + 1):
        if j < NCH:
            loads[j].wait()
            eh, el = split(e_ref[CH * j : CH * (j + 1), :])
            e3 = jnp.concatenate([eh, el, eh], axis=1)
            for q in range(0, PROT, 256):
                mats[j][q : q + 256, :] = nt(p3_ref[q : q + 256, :], e3)
        if j >= 1:
            v = mats[j - 1][...]
            m = deep(v, jnp.max)
            lam[:, CH * (j - 1) : CH * j] = m + jnp.log2(deep(jnp.exp2(v - m), jnp.sum))

    pl.semaphore_wait(barrier, len(everyone))

    def await_bytes(ref, sem):
        pltpu.make_async_copy(ref, ref, sem).wait()

    def send(src, dst, ssem, rsem, device):
        pltpu.make_async_remote_copy(src, dst, ssem, rsem, device_id=device, device_id_type=MESH).start()

    def row_exchange(n, vec, combine):
        vec_row[n] = vec
        send(vec_row.at[n], pair_buf.at[n], ps.at[n], pr.at[n], pair_dev)
        await_bytes(pair_buf.at[n], pr.at[n])
        z_buf[n, z] = combine([vec, pair_buf[n]])
        for d in z_peers:
            send(z_buf.at[n, z], z_buf.at[n, z], zs.at[n], zr.at[n], z_dev(d))
        await_bytes(vec_row.at[n], ps.at[n])
        seven = z_buf.at[n, pl.ds(0, NZ - 1)]
        await_bytes(seven, zr.at[n])
        await_bytes(seven, zs.at[n])
        return combine([z_buf[n, d] for d in range(NZ)])

    def col_send(n, vec):
        xy_buf[n, dp] = vec
        for p in xy_peers:
            send(xy_buf.at[n, dp], xy_buf.at[n, dp], cs.at[n], cr.at[n], xy_dev(*p))

    def col_wait(n, combine):
        rest = xy_buf.at[n, pl.ds(0, NDP - 1)]
        await_bytes(rest, cr.at[n])
        await_bytes(rest, cs.at[n])
        return combine([xy_buf[n, d] for d in range(NDP)])

    def to_lanes(src, reduce):
        return jnp.concatenate(
            [reduce(src[128 * a : 128 * (a + 1), :].T, axis=0, keepdims=True) for a in range(PROT // 128)], axis=0)

    def to_wide(dst, vec):
        for a in range(PROT // 128):
            dst[128 * a : 128 * (a + 1), :] = jnp.broadcast_to(vec[a : a + 1, :], (128, 128)).T

    def cut(j):
        return slice(CH * j, CH * (j + 1))

    def blocks(step, carry=0):
        return lax.fori_loop(
            0, PROT // BLK, lambda g, a: step(pl.ds(pl.multiple_of(g * BLK, BLK), BLK), a), carry)

    def row_sums():
        def step(r, acc):
            v = twice(wide[r, :])
            return tuple(a + jnp.sum((m[r, :] * v).reshape(BLK // 8, 8, CH), axis=0) for a, m in zip(acc, mats))

        acc = blocks(step, tuple(jnp.zeros((8, CH), F32) for _ in mats))
        return jnp.sum(jnp.concatenate(acc, axis=1), axis=0, keepdims=True)

    def col_sums(u):
        rb_ref[...] = u

        def step(r, a):
            part[r, :] = tree([fold(m[r, :] * rb_ref[:, cut(j)], jnp.add) for j, m in enumerate(mats)], jnp.add)
            return a

        blocks(step)
        return to_lanes(part, jnp.sum)

    rb_ref[...] = row_exchange(0, lam[...], log_sum)

    def peak_step(r, a):
        part[r, :] = tree([fold(m[r, :] - rb_ref[:, cut(j)], jnp.maximum) for j, m in enumerate(mats)], jnp.maximum)
        return a

    blocks(peak_step)
    peak = to_lanes(part, jnp.max)
    to_wide(peaks, peak)

    def exp_step(r, a):
        pk = twice(peaks[r, :])
        s = []
        for j, m in enumerate(mats):
            b = jnp.exp2(m[r, :] - rb_ref[:, cut(j)] - pk)
            m[r, :] = b
            s.append(fold(b, jnp.add))
        part[r, :] = tree(s, jnp.add)
        return a

    blocks(exp_step)
    col_send(0, peak + jnp.log2(to_lanes(part, jnp.sum)))

    def halves(r, a):
        for j, m in enumerate(mats):
            h, l = split(m[r, :])
            hi_ref[r, cut(j)] = h
            lo_ref[r, cut(j)] = l
        return a

    blocks(halves)

    g_log = col_wait(0, log_sum)
    w = jnp.exp2(peak - g_log)
    ratio = TOTAL_ROWS / TOTAL_PROT
    to_wide(wide, w * ratio)
    u = 1.0 / row_exchange(1, row_sums(), total)
    col_send(1, w * col_sums(u))
    mass = col_wait(1, total)
    to_wide(wide, w * ratio / mass)
    u = 1.0 / row_exchange(2, row_sums(), total)

    for a in range(ROWS // 128):
        ewide[128 * a : 128 * (a + 1), :] = jnp.broadcast_to(u[:, 128 * a : 128 * (a + 1)], (128, 128)).T
    to_wide(wide, w)

    def scale_rows(g, a):
        rows = pl.ds(pl.multiple_of(g * 128, 128), 128)
        h, l = split(e_ref[rows, :] * twice(ewide[rows, :]))
        eh2[rows, :] = h
        el2[rows, :] = l
        return a

    lax.fori_loop(0, ROWS // 128, scale_rows, 0)

    def rows_of(base, unit, index):
        return pl.ds(pl.multiple_of(base + unit * index, 8), unit)

    n_x, n_y = (NX, x, x_peers, lambda d: xy_dev(d, 0)), (NY, y, y_peers, lambda d: xy_dev(0, d))

    def plan(p):
        base, size, first = PARTS[p]
        one, two = (n_x, n_y) if first == "x" else (n_y, n_x)
        return base, size, one, two, size // one[0], size // NDP

    def scatter_one(p):
        base, size, (n, me, peers, dev), _, c1, _ = plan(p)
        for d in peers:
            send(sums.at[rows_of(base, c1, (me + d) % n)], b1s[p].at[me], fs.at[4 * p], fr.at[4 * p], dev(d))
        b1s[p][me] = sums[rows_of(base, c1, me), :]

    def scatter_two(p):
        _, size, (n1, _, _, _), (n, me, peers, dev), c1, c2 = plan(p)
        await_bytes(b1s[p].at[pl.ds(0, n1 - 1)], fr.at[4 * p])
        mids[p][...] = total([b1s[p][d] for d in range(n1)])
        for d in peers:
            send(mids[p].at[rows_of(0, c2, (me + d) % n)], b2s[p].at[me], fs.at[4 * p + 1], fr.at[4 * p + 1], dev(d))
        b2s[p][me] = mids[p][rows_of(0, c2, me), :]

    def gather_one(p):
        base, size, (_, me1, _, _), (n, me, peers, dev), c1, c2 = plan(p)
        await_bytes(b2s[p].at[pl.ds(0, n - 1)], fr.at[4 * p + 1])
        own = rows_of(base, c2, me1 * n + me)
        v = total([b2s[p][d] for d in range(n)]) * twice(part[own, :])
        out[own, :] = v * lax.rsqrt(jnp.mean(v * v, axis=1, keepdims=True) + 1e-06)
        for d in peers:
            send(out.at[own], out.at[own], fs.at[4 * p + 2], fr.at[4 * p + 2], dev(d))

    def gather_two(p):
        base, size, (_, me, peers, dev), _, c1, c2 = plan(p)
        await_bytes(out.at[pl.ds(0, c1 - c2)], fr.at[4 * p + 2])
        mid = rows_of(base, c1, me)
        for d in peers:
            send(out.at[mid], out.at[mid], fs.at[4 * p + 3], fr.at[4 * p + 3], dev(d))

    for p, (base, size, _) in enumerate(PARTS):
        rows = pl.ds(base, size)
        h = hi_ref[rows, :]
        acc = nn(h, eh2[...]) + nn(h, el2[...]) + nn(lo_ref[rows, :], eh2[...])
        sums[rows, :] = acc * twice(wide[rows, :])
        scatter_one(p)
        if p == 1:
            col_send(2, w * col_sums(u))

    scatter_two(1)
    scatter_two(2)
    scatter_two(0)
    scatter_two(3)
    mass = col_wait(2, total)
    pot_ref[...] = ((math.log(TOTAL_ROWS / TOTAL_PROT) - LN2 * g_log) - jnp.log(mass)).reshape(pot_ref.shape)
    to_wide(part, 1.0 / mass)
    for p in (1, 0, 2, 3):
        gather_one(p)
    for p in (0, 1, 2, 3):
        gather_two(p)
    for p in (0, 1, 2, 3):
        _, size, _, _, c1, c2 = plan(p)
        await_bytes(out.at[pl.ds(0, size - c1)], fr.at[4 * p + 3])
        for n, sent in enumerate((size - c1, c1 - c2, c1 - c2, size - c1)):
            await_bytes(sums.at[pl.ds(0, sent)], fs.at[4 * p + n])


def body(embeddings, prototypes):
    vm = pltpu.VMEM
    dma = pltpu.SemaphoreType.DMA
    counts = [(NX, NY) if first == "x" else (NY, NX) for _, _, first in PARTS]
    sizes = [size for _, size, _ in PARTS]
    new_protos, pot = pl.pallas_call(
        kernel,
        out_shape=(pltpu.VMEM((PROT, DW), F32), pltpu.VMEM((PROT,), F32)),
        in_specs=[pl.BlockSpec(memory_space=pl.ANY)] * 2,
        out_specs=(pl.BlockSpec(memory_space=vm), pl.BlockSpec(memory_space=vm)),
        scratch_shapes=[
            vm((ROWS, DW), F32),
            vm((PROT, DW), F32),
            vm((PROT, 3 * DW), BF16),
            *[vm((PROT, CH), F32) for _ in range(NCH)],
            *[vm((a, s // a, DW), F32) for (a, _), s in zip(counts, sizes)],
            *[vm((s // a, DW), F32) for (a, _), s in zip(counts, sizes)],
            *[vm((b, s // NDP, DW), F32) for (_, b), s in zip(counts, sizes)],
            vm((PROT, ROWS), BF16),
            vm((PROT, ROWS), BF16),
            vm((PROT, 128), F32),
            vm((PROT, 128), F32),
            vm((PROT, 128), F32),
            vm((ROWS, 128), F32),
            vm((ROWS, DW), BF16),
            vm((ROWS, DW), BF16),
            vm((1, ROWS), F32),
            vm((1, ROWS), F32),
            vm((3, 1, ROWS), F32),
            vm((3, NZ, 1, ROWS), F32),
            vm((3, NDP, 8, 128), F32),
            vm((3, 1, ROWS), F32),
            vm((PROT, DW), F32),
            dma((NCH + 1,)),
            dma((3,)), dma((3,)),
            dma((3,)), dma((3,)),
            dma((3,)), dma((3,)),
            dma((4 * len(PARTS),)), dma((4 * len(PARTS),)),
        ],
        compiler_params=pltpu.CompilerParams(
            collective_id=0, has_side_effects=True, vmem_limit_bytes=56 * 1024 * 1024),
        name="sinkhorn",
    )(embeddings, prototypes)
    return new_protos, pot


def solution(mesh):
    in_specs = (P("dp", None), P("bucket", None))
    out_specs = (P("bucket", None), P("bucket"))
    return jax.shard_map(body, mesh=mesh, in_specs=in_specs, out_specs=out_specs, check_vma=False)
```

```python
import functools
import math

import jax
import jax.numpy as jnp
from jax import lax
from jax.experimental import pallas as pl
from jax.experimental.pallas import tpu as pltpu
from jax.sharding import PartitionSpec as P

NX, NY, NZ, NC = 4, 8, 8, 2
NDP = NX * NY
MESH = pl.DeviceIdType.MESH
F32 = jnp.float32
BF16 = jnp.bfloat16
LN2 = math.log(2.0)

ROWS = 2048
PROT = 1024
DW = 256
TOTAL_ROWS = ROWS * NDP
TOTAL_PROT = PROT * NZ * NC

CH = 256
NCH = ROWS // CH
HALF = ROWS // 2
NB = NZ * NC
PARTS = ((0, 256, "y"), (256, 256, "x"), (512, 256, "x"), (768, 256, "x"))


def split(x):
    hi = x.astype(BF16)
    return hi, (x - hi.astype(F32)).astype(BF16)


def nt(a, b):
    return lax.dot_general(a, b, (((1,), (1,)), ((), ())), preferred_element_type=F32)


def nn(a, b):
    return lax.dot_general(a, b, (((1,), (0,)), ((), ())), preferred_element_type=F32)


def tree(parts, op):
    while len(parts) > 1:
        parts = [op(a, b) for a, b in zip(parts[::2], parts[1::2])]
    return parts[0]


def twice(v):
    return jnp.concatenate([v, v], axis=1)


def fold(v, op):
    return op(v[:, :128], v[:, 128:])


def log_sum(terms):
    peak = functools.reduce(jnp.maximum, terms)
    mass = functools.reduce(jnp.add, [jnp.exp2(t - peak) for t in terms])
    return peak + jnp.log2(mass)


def total(terms):
    return functools.reduce(jnp.add, terms)


def kernel(*refs):
    (e_hbm, p_hbm, out, pot_ref, e_ref, p_ref, p3_ref), refs = refs[:7], refs[7:]
    mats, refs = refs[:NCH], refs[NCH:]
    b1s, refs = refs[: len(PARTS)], refs[len(PARTS) :]
    mids, refs = refs[: len(PARTS)], refs[len(PARTS) :]
    b2s, refs = refs[: len(PARTS)], refs[len(PARTS) :]
    (hi_ref, lo_ref, part, wide, peaks, eh2, el2, lam, rb_ref, z_buf, xy_buf, c3x, c3y, sums,
     load_sem, zs, zr, cs, cr, fs, fr) = refs
    dp, bk = lax.axis_index("dp"), lax.axis_index("bucket")
    x, y = dp // NY, dp % NY
    z, c = bk // NC, bk % NC

    loads_e, loads_p = [], []
    for j in range(NCH):
        rows = pl.ds(CH * j, CH)
        loads_e.append(pltpu.make_async_copy(e_hbm.at[rows], e_ref.at[rows], load_sem.at[j]))
    for q in range(PROT // CH):
        rows = pl.ds(CH * q, CH)
        loads_p.append(pltpu.make_async_copy(p_hbm.at[rows], p_ref.at[rows], load_sem.at[NCH + q]))
    for copy in loads_e[:1] + loads_p + loads_e[1:]:
        copy.start()

    def bk_dev(d):
        return (dp, (bk + d) % NB)

    def xy_dev(dx, dy):
        return (((x + dx) % NX) * NY + (y + dy) % NY, bk)

    xy_peers = sorted(
        [(dx, dy) for dx in range(NX) for dy in range(NY) if dx or dy],
        key=lambda p: -(min(p[0], NX - p[0]) + min(p[1], NY - p[1])),
    )
    bk_peers = sorted(range(1, NB), key=lambda d: -min(d, NB - d))
    x_peers, y_peers = [2, 1, 3], [4, 3, 5, 2, 6, 1, 7]

    barrier = pltpu.get_barrier_semaphore()
    everyone = [bk_dev(d) for d in bk_peers] + [xy_dev(*p) for p in xy_peers]
    for d in everyone:
        pl.semaphore_signal(barrier, 1, device_id=d, device_id_type=MESH)

    def await_bytes(ref, sem):
        pltpu.make_async_copy(ref, ref, sem).wait()

    def send(src, dst, ssem, rsem, device):
        pltpu.make_async_remote_copy(src, dst, ssem, rsem, device_id=device, device_id_type=MESH).start()

    def row_send(n, h, vec):
        z_buf[n, h, bk] = vec
        for d in bk_peers:
            send(z_buf.at[n, h, bk], z_buf.at[n, h, bk], zs.at[2 * n + h], zr.at[2 * n + h], bk_dev(d))

    def row_wait(n, h, combine):
        rest = z_buf.at[n, h, pl.ds(0, NB - 1)]
        await_bytes(rest, zr.at[2 * n + h])
        await_bytes(rest, zs.at[2 * n + h])
        return combine([z_buf[n, h, d] for d in range(NB)])

    def deep(v, op):
        v = op(op(v.reshape(PROT // 32, 4, 8, CH), axis=0), axis=0)
        return op(v, axis=0, keepdims=True)

    for j in range(NCH + 1):
        if j < NCH:
            loads_e[j].wait()
            eh, el = split(e_ref[CH * j : CH * (j + 1), :])
            e3 = jnp.concatenate([eh, el, eh], axis=1)
            for q in range(PROT // CH):
                r = slice(CH * q, CH * (q + 1))
                if j == 0:
                    loads_p[q].wait()
                    ph, plo = split(p_ref[r, :] * F32(2.0 / math.sqrt(DW) / LN2))
                    p3_ref[r, 0:DW] = ph
                    p3_ref[r, DW : 2 * DW] = ph
                    p3_ref[r, 2 * DW :] = plo
                mats[j][r, :] = nt(p3_ref[r, :], e3)
        if j >= 1:
            v = mats[j - 1][...]
            m = deep(v, jnp.max)
            lam[:, CH * (j - 1) : CH * j] = m + jnp.log2(deep(jnp.exp2(v - m), jnp.sum))
        if j == NCH // 2:
            pl.semaphore_wait(barrier, len(everyone))
            row_send(0, 0, lam[:, :HALF])
    row_send(0, 1, lam[:, HALF:])

    def col_send(n, vec):
        xy_buf[n, dp] = vec
        for p in xy_peers:
            send(xy_buf.at[n, dp], xy_buf.at[n, dp], cs.at[n], cr.at[n], xy_dev(*p))

    def col_wait(n, combine):
        rest = xy_buf.at[n, pl.ds(0, NDP - 1)]
        await_bytes(rest, cr.at[n])
        await_bytes(rest, cs.at[n])
        return combine([xy_buf[n, d] for d in range(NDP)])

    def to_row(v, reduce):
        return reduce(v.T, axis=0, keepdims=True)

    def to_tile(row):
        return jnp.broadcast_to(row, (128, 128)).T

    def cut(j):
        return slice(CH * j, CH * (j + 1))

    blocks = [slice(128 * a, 128 * (a + 1)) for a in range(PROT // 128)]
    groups = (range(NCH // 2), range(NCH // 2, NCH))

    def half(h):
        return slice(HALF * h, HALF * (h + 1))

    def row_sums(h, vec=None):
        acc = [jnp.zeros((8, CH), F32) for _ in groups[h]]
        for a, r in enumerate(blocks):
            if vec is not None:
                wide[r, :] = to_tile(vec[a : a + 1, :])
            v = twice(wide[r, :])
            acc = [t + jnp.sum((mats[j][r, :] * v).reshape(16, 8, CH), axis=0) for t, j in zip(acc, groups[h])]
        return jnp.sum(jnp.concatenate(acc, axis=1), axis=0, keepdims=True)

    def row_step(n, vec):
        row_send(n, 0, row_sums(0, vec))
        row_send(n, 1, row_sums(1))

    def col_terms(r, js):
        return tree([fold(mats[j][r, :] * rb_ref[:, cut(j)], jnp.add) for j in js], jnp.add)

    def peak_terms(r, js):
        return tree([fold(mats[j][r, :] - rb_ref[:, cut(j)], jnp.maximum) for j in js], jnp.maximum)

    rb_ref[:, half(0)] = row_wait(0, 0, log_sum)
    for r in blocks:
        part[r, :] = peak_terms(r, groups[0])
    rb_ref[:, half(1)] = row_wait(0, 1, log_sum)
    rows_of_peaks = []
    for r in blocks:
        row = to_row(jnp.maximum(part[r, :], peak_terms(r, groups[1])), jnp.max)
        rows_of_peaks.append(row)
        peaks[r, :] = to_tile(row)
    peak = jnp.concatenate(rows_of_peaks, axis=0)

    masses = []
    for r in blocks:
        pk = twice(peaks[r, :])
        terms = []
        for j, m in enumerate(mats):
            b = jnp.exp2(m[r, :] - rb_ref[:, cut(j)] - pk)
            m[r, :] = b
            terms.append(fold(b, jnp.add))
        masses.append(to_row(tree(terms, jnp.add), jnp.sum))
    col_send(0, peak + jnp.log2(jnp.concatenate(masses, axis=0)))

    def halves(g, carry):
        r = pl.ds(pl.multiple_of(g * 64, 64), 64)
        for j, m in enumerate(mats):
            h, l = split(m[r, :])
            hi_ref[r, cut(j)] = h
            lo_ref[r, cut(j)] = l
        return carry

    lax.fori_loop(0, PROT // 64, halves, 0)

    g_log = col_wait(0, log_sum)
    w = jnp.exp2(peak - g_log)
    ratio = TOTAL_ROWS / TOTAL_PROT
    row_step(1, w * ratio)
    for a, r in enumerate(blocks):
        peaks[r, :] = to_tile(w[a : a + 1, :])
    rb_ref[:, half(0)] = 1.0 / row_wait(1, 0, total)
    for r in blocks:
        part[r, :] = col_terms(r, groups[0])
    rb_ref[:, half(1)] = 1.0 / row_wait(1, 1, total)
    col_send(1, w * jnp.concatenate([to_row(part[r, :] + col_terms(r, groups[1]), jnp.sum) for r in blocks], axis=0))
    row_step(2, w * ratio / col_wait(1, total))

    def scale_rows(h):
        for a in range(8 * h, 8 * h + 8):
            r = slice(128 * a, 128 * (a + 1))
            t, l = split(e_ref[r, :] * twice(to_tile(rb_ref[:, r])))
            eh2[r, :] = t
            el2[r, :] = l

    def product(r, k):
        h = hi_ref[r, k]
        return nn(h, eh2[k, :]) + nn(h, el2[k, :]) + nn(lo_ref[r, k], eh2[k, :])

    rb_ref[:, half(0)] = 1.0 / row_wait(2, 0, total)
    scale_rows(0)
    first = slice(PARTS[0][0], PARTS[0][0] + PARTS[0][1])
    sums[first, :] = product(first, half(0))
    rb_ref[:, half(1)] = 1.0 / row_wait(2, 1, total)
    scale_rows(1)

    def rows_of(base, unit, index):
        return pl.ds(pl.multiple_of(base + unit * index, 8), unit)

    n_x, n_y = (NX, x, x_peers, lambda d: xy_dev(d, 0)), (NY, y, y_peers, lambda d: xy_dev(0, d))

    def plan(p):
        base, size, first = PARTS[p]
        one, two = (n_x, n_y) if first == "x" else (n_y, n_x)
        return base, size, one, two, size // one[0], size // NDP

    def scatter_one(p):
        base, size, (n, me, peers, dev), _, c1, _ = plan(p)
        for d in peers:
            send(sums.at[rows_of(base, c1, (me + d) % n)], b1s[p].at[me], fs.at[4 * p], fr.at[4 * p], dev(d))
        b1s[p][me] = sums[rows_of(base, c1, me), :]

    def scatter_two(p):
        _, size, (n1, _, _, _), (n, me, peers, dev), c1, c2 = plan(p)
        await_bytes(b1s[p].at[pl.ds(0, n1 - 1)], fr.at[4 * p])
        mids[p][...] = total([b1s[p][d] for d in range(n1)])
        for d in peers:
            send(mids[p].at[rows_of(0, c2, (me + d) % n)], b2s[p].at[me], fs.at[4 * p + 1], fr.at[4 * p + 1], dev(d))
        b2s[p][me] = mids[p][rows_of(0, c2, me), :]

    def gather_one(p):
        base, size, (_, me1, _, _), (n, me, peers, dev), c1, c2 = plan(p)
        await_bytes(b2s[p].at[pl.ds(0, n - 1)], fr.at[4 * p + 1])
        own = rows_of(base, c2, me1 * n + me)
        v = total([b2s[p][d] for d in range(n)]) * twice(part[own, :])
        out[own, :] = v * lax.rsqrt(jnp.mean(v * v, axis=1, keepdims=True) + 1e-06)
        for d in peers:
            send(out.at[own], out.at[own], fs.at[4 * p + 2], fr.at[4 * p + 2], dev(d))

    def gather_two(p):
        base, size, (_, me, peers, dev), _, c1, c2 = plan(p)
        await_bytes(out.at[pl.ds(0, c1 - c2)], fr.at[4 * p + 2])
        mid = rows_of(base, c1, me)
        for d in peers:
            send(out.at[mid], out.at[mid], fs.at[4 * p + 3], fr.at[4 * p + 3], dev(d))

    for p, (base, size, _) in enumerate(PARTS):
        rows = slice(base, base + size)
        acc = sums[rows, :] + product(rows, half(1)) if p == 0 else product(rows, slice(0, ROWS))
        sums[rows, :] = acc * twice(peaks[rows, :])
        scatter_one(p)
        if p == 1:
            c3x[x] = w * jnp.concatenate([to_row(col_terms(r, range(NCH)), jnp.sum) for r in blocks], axis=0)
            for d in x_peers:
                send(c3x.at[x], c3x.at[x], cs.at[2], cr.at[2], xy_dev(d, 0))

    scatter_two(1)
    await_bytes(c3x.at[pl.ds(0, NX - 1)], cr.at[2])
    c3y[y] = total([c3x[d] for d in range(NX)])
    for d in y_peers:
        send(c3y.at[y], c3y.at[y], cs.at[3], cr.at[3], xy_dev(0, d))
    scatter_two(2)
    scatter_two(0)
    scatter_two(3)
    await_bytes(c3y.at[pl.ds(0, NY - 1)], cr.at[3])
    mass = total([c3y[d] for d in range(NY)])
    pot_ref[...] = ((math.log(TOTAL_ROWS / TOTAL_PROT) - LN2 * g_log) - jnp.log(mass)).reshape(pot_ref.shape)
    for a, r in enumerate(blocks):
        part[r, :] = to_tile(1.0 / mass[a : a + 1, :])
    await_bytes(c3x.at[pl.ds(0, NX - 1)], cs.at[2])
    await_bytes(c3y.at[pl.ds(0, NY - 1)], cs.at[3])
    for p in (1, 0, 2, 3):
        gather_one(p)
    for p in (0, 1, 2, 3):
        gather_two(p)
    for p in (0, 1, 2, 3):
        _, size, _, _, c1, c2 = plan(p)
        await_bytes(out.at[pl.ds(0, size - c1)], fr.at[4 * p + 3])
        for n, sent in enumerate((size - c1, c1 - c2, c1 - c2, size - c1)):
            await_bytes(sums.at[pl.ds(0, sent)], fs.at[4 * p + n])


def body(embeddings, prototypes):
    vm = pltpu.VMEM
    dma = pltpu.SemaphoreType.DMA
    counts = [(NX, NY) if first == "x" else (NY, NX) for _, _, first in PARTS]
    sizes = [size for _, size, _ in PARTS]
    new_protos, pot = pl.pallas_call(
        kernel,
        out_shape=(pltpu.VMEM((PROT, DW), F32), pltpu.VMEM((PROT,), F32)),
        in_specs=[pl.BlockSpec(memory_space=pl.ANY)] * 2,
        out_specs=(pl.BlockSpec(memory_space=vm), pl.BlockSpec(memory_space=vm)),
        scratch_shapes=[
            vm((ROWS, DW), F32),
            vm((PROT, DW), F32),
            vm((PROT, 3 * DW), BF16),
            *[vm((PROT, CH), F32) for _ in range(NCH)],
            *[vm((a, s // a, DW), F32) for (a, _), s in zip(counts, sizes)],
            *[vm((s // a, DW), F32) for (a, _), s in zip(counts, sizes)],
            *[vm((b, s // NDP, DW), F32) for (_, b), s in zip(counts, sizes)],
            vm((PROT, ROWS), BF16),
            vm((PROT, ROWS), BF16),
            vm((PROT, 128), F32),
            vm((PROT, 128), F32),
            vm((PROT, 128), F32),
            vm((ROWS, DW), BF16),
            vm((ROWS, DW), BF16),
            vm((1, ROWS), F32),
            vm((1, ROWS), F32),
            vm((3, 2, NB, 1, HALF), F32),
            vm((2, NDP, 8, 128), F32),
            vm((NX, 8, 128), F32),
            vm((NY, 8, 128), F32),
            vm((PROT, DW), F32),
            dma((NCH + PROT // CH,)),
            dma((6,)), dma((6,)),
            dma((4,)), dma((4,)),
            dma((4 * len(PARTS),)), dma((4 * len(PARTS),)),
        ],
        compiler_params=pltpu.CompilerParams(
            collective_id=0, has_side_effects=True, vmem_limit_bytes=56 * 1024 * 1024),
        name="sinkhorn",
    )(embeddings, prototypes)
    return new_protos, pot


def solution(mesh):
    in_specs = (P("dp", None), P("bucket", None))
    out_specs = (P("bucket", None), P("bucket"))
    return jax.shard_map(body, mesh=mesh, in_specs=in_specs, out_specs=out_specs, check_vma=False)
```

```python
import functools
import math

import jax
import jax.numpy as jnp
from jax import lax
from jax.experimental import pallas as pl
from jax.experimental.pallas import tpu as pltpu
from jax.sharding import PartitionSpec as P

NX, NY, NZ, NC = 4, 8, 8, 2
NDP = NX * NY
MESH = pl.DeviceIdType.MESH
F32 = jnp.float32
BF16 = jnp.bfloat16
LN2 = math.log(2.0)

ROWS = 2048
PROT = 1024
DW = 256
TOTAL_ROWS = ROWS * NDP
TOTAL_PROT = PROT * NZ * NC

CH = 256
NCH = ROWS // CH
HALF = ROWS // 2
NB = NZ * NC
PARTS = ((0, 256, "y"), (256, 256, "x"), (512, 256, "x"), (768, 128, "x"), (896, 128, "x"))


def split(x):
    hi = x.astype(BF16)
    return hi, (x - hi.astype(F32)).astype(BF16)


def nt(a, b):
    return lax.dot_general(a, b, (((1,), (1,)), ((), ())), preferred_element_type=F32)


def nn(a, b):
    return lax.dot_general(a, b, (((1,), (0,)), ((), ())), preferred_element_type=F32)


def tree(parts, op):
    while len(parts) > 1:
        parts = [op(a, b) for a, b in zip(parts[::2], parts[1::2])]
    return parts[0]


def twice(v):
    return jnp.concatenate([v, v], axis=1)


def fold(v, op):
    return op(v[:, :128], v[:, 128:])


def log_sum(terms):
    peak = functools.reduce(jnp.maximum, terms)
    mass = functools.reduce(jnp.add, [jnp.exp2(t - peak) for t in terms])
    return peak + jnp.log2(mass)


def total(terms):
    return functools.reduce(jnp.add, terms)


def kernel(*refs):
    (e_hbm, p_hbm, out, pot_ref, e_ref, p_ref, p3_ref), refs = refs[:7], refs[7:]
    mats, refs = refs[:NCH], refs[NCH:]
    b1s, refs = refs[: len(PARTS)], refs[len(PARTS) :]
    mids, refs = refs[: len(PARTS)], refs[len(PARTS) :]
    b2s, refs = refs[: len(PARTS)], refs[len(PARTS) :]
    (hi_ref, lo_ref, part, wide, peaks, eh2, el2, lam, rb_ref, z_buf, xy_buf, c3x, c3y, sums, raw,
     load_sem, zs, zr, cs, cr, fs, fr) = refs
    dp, bk = lax.axis_index("dp"), lax.axis_index("bucket")
    x, y = dp // NY, dp % NY
    z, c = bk // NC, bk % NC

    loads_e, loads_p = [], []
    for j in range(NCH):
        rows = pl.ds(CH * j, CH)
        loads_e.append(pltpu.make_async_copy(e_hbm.at[rows], e_ref.at[rows], load_sem.at[j]))
    for q in range(PROT // CH):
        rows = pl.ds(CH * q, CH)
        loads_p.append(pltpu.make_async_copy(p_hbm.at[rows], p_ref.at[rows], load_sem.at[NCH + q]))
    for copy in loads_e[:1] + loads_p + loads_e[1:]:
        copy.start()

    def bk_dev(d):
        return (dp, (bk + d) % NB)

    def xy_dev(dx, dy):
        return (((x + dx) % NX) * NY + (y + dy) % NY, bk)

    xy_peers = sorted(
        [(dx, dy) for dx in range(NX) for dy in range(NY) if dx or dy],
        key=lambda p: -(min(p[0], NX - p[0]) + min(p[1], NY - p[1])),
    )
    bk_peers = sorted(range(1, NB), key=lambda d: -min(d, NB - d))
    x_peers, y_peers = [2, 1, 3], [4, 3, 5, 2, 6, 1, 7]

    barrier = pltpu.get_barrier_semaphore()
    everyone = [bk_dev(d) for d in bk_peers] + [xy_dev(*p) for p in xy_peers]
    for d in everyone:
        pl.semaphore_signal(barrier, 1, device_id=d, device_id_type=MESH)

    def await_bytes(ref, sem):
        pltpu.make_async_copy(ref, ref, sem).wait()

    def send(src, dst, ssem, rsem, device):
        pltpu.make_async_remote_copy(src, dst, ssem, rsem, device_id=device, device_id_type=MESH).start()

    def row_send(n, h, vec):
        z_buf[n, h, bk] = vec
        for d in bk_peers:
            send(z_buf.at[n, h, bk], z_buf.at[n, h, bk], zs.at[2 * n + h], zr.at[2 * n + h], bk_dev(d))

    def row_wait(n, h, combine):
        rest = z_buf.at[n, h, pl.ds(0, NB - 1)]
        await_bytes(rest, zr.at[2 * n + h])
        await_bytes(rest, zs.at[2 * n + h])
        return combine([z_buf[n, h, d] for d in range(NB)])

    def deep(v, op):
        v = op(op(v.reshape(PROT // 32, 4, 8, CH), axis=0), axis=0)
        return op(v, axis=0, keepdims=True)

    for j in range(NCH + 1):
        if j < NCH:
            loads_e[j].wait()
            eh, el = split(e_ref[CH * j : CH * (j + 1), :])
            e3 = jnp.concatenate([eh, el, eh], axis=1)
            for q in range(PROT // CH):
                r = slice(CH * q, CH * (q + 1))
                if j == 0:
                    loads_p[q].wait()
                    ph, plo = split(p_ref[r, :] * F32(2.0 / math.sqrt(DW) / LN2))
                    p3_ref[r, 0:DW] = ph
                    p3_ref[r, DW : 2 * DW] = ph
                    p3_ref[r, 2 * DW :] = plo
                mats[j][r, :] = nt(p3_ref[r, :], e3)
        if j >= 1:
            v = mats[j - 1][...]
            m = deep(v, jnp.max)
            lam[:, CH * (j - 1) : CH * j] = m + jnp.log2(deep(jnp.exp2(v - m), jnp.sum))
        if j == NCH // 2:
            pl.semaphore_wait(barrier, len(everyone))
            row_send(0, 0, lam[:, :HALF])
    row_send(0, 1, lam[:, HALF:])

    def col_send(n, vec):
        xy_buf[n, dp] = vec
        for p in xy_peers:
            send(xy_buf.at[n, dp], xy_buf.at[n, dp], cs.at[n], cr.at[n], xy_dev(*p))

    def col_wait(n, combine):
        rest = xy_buf.at[n, pl.ds(0, NDP - 1)]
        await_bytes(rest, cr.at[n])
        await_bytes(rest, cs.at[n])
        return combine([xy_buf[n, d] for d in range(NDP)])

    def to_row(v, reduce):
        return reduce(v.T, axis=0, keepdims=True)

    def to_tile(row):
        return jnp.broadcast_to(row, (128, 128)).T

    def cut(j):
        return slice(CH * j, CH * (j + 1))

    blocks = [slice(128 * a, 128 * (a + 1)) for a in range(PROT // 128)]
    groups = (range(NCH // 2), range(NCH // 2, NCH))

    def half(h):
        return slice(HALF * h, HALF * (h + 1))

    def row_sums(h, vec=None):
        acc = [jnp.zeros((8, CH), F32) for _ in groups[h]]
        for a, r in enumerate(blocks):
            if vec is not None:
                wide[r, :] = to_tile(vec[a : a + 1, :])
            v = twice(wide[r, :])
            acc = [t + jnp.sum((mats[j][r, :] * v).reshape(16, 8, CH), axis=0) for t, j in zip(acc, groups[h])]
        return jnp.sum(jnp.concatenate(acc, axis=1), axis=0, keepdims=True)

    def row_step(n, vec):
        row_send(n, 0, row_sums(0, vec))
        row_send(n, 1, row_sums(1))

    def col_terms(r, js):
        return tree([fold(mats[j][r, :] * rb_ref[:, cut(j)], jnp.add) for j in js], jnp.add)

    def peak_terms(r, js):
        return tree([fold(mats[j][r, :] - rb_ref[:, cut(j)], jnp.maximum) for j in js], jnp.maximum)

    rb_ref[:, half(0)] = row_wait(0, 0, log_sum)
    for r in blocks:
        part[r, :] = peak_terms(r, groups[0])
    rb_ref[:, half(1)] = row_wait(0, 1, log_sum)
    rows_of_peaks = []
    for r in blocks:
        row = to_row(jnp.maximum(part[r, :], peak_terms(r, groups[1])), jnp.max)
        rows_of_peaks.append(row)
        peaks[r, :] = to_tile(row)
    peak = jnp.concatenate(rows_of_peaks, axis=0)

    masses = []
    for r in blocks:
        pk = twice(peaks[r, :])
        terms = []
        for j, m in enumerate(mats):
            b = jnp.exp2(m[r, :] - rb_ref[:, cut(j)] - pk)
            m[r, :] = b
            terms.append(fold(b, jnp.add))
        masses.append(to_row(tree(terms, jnp.add), jnp.sum))
    col_send(0, peak + jnp.log2(jnp.concatenate(masses, axis=0)))

    def halves(g, carry):
        r = pl.ds(pl.multiple_of(g * 64, 64), 64)
        for j, m in enumerate(mats):
            h, l = split(m[r, :])
            hi_ref[r, cut(j)] = h
            lo_ref[r, cut(j)] = l
        return carry

    lax.fori_loop(0, PROT // 64, halves, 0)

    g_log = col_wait(0, log_sum)
    w = jnp.exp2(peak - g_log)
    ratio = TOTAL_ROWS / TOTAL_PROT
    row_step(1, w * ratio)
    for a, r in enumerate(blocks):
        peaks[r, :] = to_tile(w[a : a + 1, :])
    rb_ref[:, half(0)] = 1.0 / row_wait(1, 0, total)
    for r in blocks:
        part[r, :] = col_terms(r, groups[0])
    rb_ref[:, half(1)] = 1.0 / row_wait(1, 1, total)
    col_send(1, w * jnp.concatenate([to_row(part[r, :] + col_terms(r, groups[1]), jnp.sum) for r in blocks], axis=0))
    row_step(2, w * ratio / col_wait(1, total))

    def scale_rows(h):
        for a in range(8 * h, 8 * h + 8):
            r = slice(128 * a, 128 * (a + 1))
            t, l = split(e_ref[r, :] * twice(to_tile(rb_ref[:, r])))
            eh2[r, :] = t
            el2[r, :] = l

    def product(r, k):
        h = hi_ref[r, k]
        return nn(h, eh2[k, :]) + nn(h, el2[k, :]) + nn(lo_ref[r, k], eh2[k, :])

    rb_ref[:, half(0)] = 1.0 / row_wait(2, 0, total)
    scale_rows(0)
    first = slice(PARTS[0][0], PARTS[0][0] + PARTS[0][1])
    sums[first, :] = product(first, half(0))
    rb_ref[:, half(1)] = 1.0 / row_wait(2, 1, total)
    scale_rows(1)

    def rows_of(base, unit, index):
        return pl.ds(pl.multiple_of(base + unit * index, 8), unit)

    n_x, n_y = (NX, x, x_peers, lambda d: xy_dev(d, 0)), (NY, y, y_peers, lambda d: xy_dev(0, d))

    def plan(p):
        base, size, first = PARTS[p]
        one, two = (n_x, n_y) if first == "x" else (n_y, n_x)
        return base, size, one, two, size // one[0]

    def piece(base, c1, n, index):
        if c1 == 8 * n:
            return rows_of(base, 8, index), pl.ds(0, DW)
        return rows_of(base, 8, index // 2), pl.ds(pl.multiple_of(128 * (index % 2), 128), 128)

    def scatter_one(p):
        base, size, (n, me, peers, dev), _, c1 = plan(p)
        for d in peers:
            send(sums.at[rows_of(base, c1, (me + d) % n)], b1s[p].at[me], fs.at[4 * p], fr.at[4 * p], dev(d))
        b1s[p][me] = sums[rows_of(base, c1, me), :]

    def scatter_two(p):
        _, size, (n1, _, _, _), (n, me, peers, dev), c1 = plan(p)
        await_bytes(b1s[p].at[pl.ds(0, n1 - 1)], fr.at[4 * p])
        mids[p][...] = total([b1s[p][d] for d in range(n1)])
        for d in peers:
            send(mids[p].at[piece(0, c1, n, (me + d) % n)], b2s[p].at[me], fs.at[4 * p + 1], fr.at[4 * p + 1], dev(d))
        b2s[p][me] = mids[p][piece(0, c1, n, me)]

    def gather_one(p):
        base, size, (_, me1, _, _), (n, me, peers, dev), c1 = plan(p)
        await_bytes(b2s[p].at[pl.ds(0, n - 1)], fr.at[4 * p + 1])
        own = piece(base + c1 * me1, c1, n, me)
        raw[own] = total([b2s[p][d] for d in range(n)])
        for d in peers:
            send(raw.at[own], raw.at[own], fs.at[4 * p + 2], fr.at[4 * p + 2], dev(d))

    def gather_two(p):
        base, size, (_, me, peers, dev), (n, _, _, _), c1 = plan(p)
        await_bytes(b2s[p].at[pl.ds(0, n - 1)], fr.at[4 * p + 2])
        mid = rows_of(base, c1, me)
        for d in peers:
            send(raw.at[mid], raw.at[mid], fs.at[4 * p + 3], fr.at[4 * p + 3], dev(d))

    def finish(p):
        base, size, (n1, _, _, _), _, c1 = plan(p)
        await_bytes(sums.at[pl.ds(0, size - c1)], fr.at[4 * p + 3])
        rows = slice(base, base + size)
        v = raw[rows, :] * twice(part[rows, :])
        out[rows, :] = v * lax.rsqrt(jnp.mean(v * v, axis=1, keepdims=True) + 1e-06)

    for p, (base, size, _) in enumerate(PARTS):
        rows = slice(base, base + size)
        acc = sums[rows, :] + product(rows, half(1)) if p == 0 else product(rows, slice(0, ROWS))
        sums[rows, :] = acc * twice(peaks[rows, :])
        scatter_one(p)

    c3x[x] = w * jnp.concatenate([to_row(col_terms(r, range(NCH)), jnp.sum) for r in blocks], axis=0)
    for d in x_peers:
        send(c3x.at[x], c3x.at[x], cs.at[2], cr.at[2], xy_dev(d, 0))

    scatter_two(1)
    scatter_two(2)
    scatter_two(0)
    await_bytes(c3x.at[pl.ds(0, NX - 1)], cr.at[2])
    c3y[y] = total([c3x[d] for d in range(NX)])
    for d in y_peers:
        send(c3y.at[y], c3y.at[y], cs.at[3], cr.at[3], xy_dev(0, d))
    scatter_two(3)
    scatter_two(4)
    gather_one(1)
    gather_one(0)
    gather_one(2)
    gather_two(0)
    gather_one(3)
    gather_one(4)
    gather_two(1)
    await_bytes(c3y.at[pl.ds(0, NY - 1)], cr.at[3])
    mass = total([c3y[d] for d in range(NY)])
    pot_ref[...] = ((math.log(TOTAL_ROWS / TOTAL_PROT) - LN2 * g_log) - jnp.log(mass)).reshape(pot_ref.shape)
    for a, r in enumerate(blocks):
        part[r, :] = to_tile(1.0 / mass[a : a + 1, :])
    gather_two(2)
    gather_two(3)
    gather_two(4)
    for p in range(len(PARTS)):
        finish(p)
    await_bytes(c3x.at[pl.ds(0, NX - 1)], cs.at[2])
    await_bytes(c3y.at[pl.ds(0, NY - 1)], cs.at[3])
    for p in range(len(PARTS)):
        _, size, _, (n, _, _, _), c1 = plan(p)
        for k in range(4):
            sent = b2s[p].at[pl.ds(0, n - 1)] if k in (1, 2) else sums.at[pl.ds(0, size - c1)]
            await_bytes(sent, fs.at[4 * p + k])


def body(embeddings, prototypes):
    vm = pltpu.VMEM
    dma = pltpu.SemaphoreType.DMA
    counts = [(NX, NY) if first == "x" else (NY, NX) for _, _, first in PARTS]
    sizes = [size for _, size, _ in PARTS]
    new_protos, pot = pl.pallas_call(
        kernel,
        out_shape=(pltpu.VMEM((PROT, DW), F32), pltpu.VMEM((PROT,), F32)),
        in_specs=[pl.BlockSpec(memory_space=pl.ANY)] * 2,
        out_specs=(pl.BlockSpec(memory_space=vm), pl.BlockSpec(memory_space=vm)),
        scratch_shapes=[
            vm((ROWS, DW), F32),
            vm((PROT, DW), F32),
            vm((PROT, 3 * DW), BF16),
            *[vm((PROT, CH), F32) for _ in range(NCH)],
            *[vm((a, s // a, DW), F32) for (a, _), s in zip(counts, sizes)],
            *[vm((s // a, DW), F32) for (a, _), s in zip(counts, sizes)],
            *[vm((b, 8, s // NDP * DW // 8), F32) for (_, b), s in zip(counts, sizes)],
            vm((PROT, ROWS), BF16),
            vm((PROT, ROWS), BF16),
            vm((PROT, 128), F32),
            vm((PROT, 128), F32),
            vm((PROT, 128), F32),
            vm((ROWS, DW), BF16),
            vm((ROWS, DW), BF16),
            vm((1, ROWS), F32),
            vm((1, ROWS), F32),
            vm((3, 2, NB, 1, HALF), F32),
            vm((2, NDP, 8, 128), F32),
            vm((NX, 8, 128), F32),
            vm((NY, 8, 128), F32),
            vm((PROT, DW), F32),
            vm((PROT, DW), F32),
            dma((NCH + PROT // CH,)),
            dma((6,)), dma((6,)),
            dma((4,)), dma((4,)),
            dma((4 * len(PARTS),)), dma((4 * len(PARTS),)),
        ],
        compiler_params=pltpu.CompilerParams(
            collective_id=0, has_side_effects=True, vmem_limit_bytes=56 * 1024 * 1024),
        name="sinkhorn",
    )(embeddings, prototypes)
    return new_protos, pot


def solution(mesh):
    in_specs = (P("dp", None), P("bucket", None))
    out_specs = (P("bucket", None), P("bucket"))
    return jax.shard_map(body, mesh=mesh, in_specs=in_specs, out_specs=out_specs, check_vma=False)
```

```python
import math

import jax
import jax.numpy as jnp
from jax import lax
from jax.experimental import pallas as pl
from jax.experimental.pallas import tpu as pltpu
from jax.sharding import PartitionSpec as P

NX, NY, NZ, NC = 4, 8, 8, 2
NDP = NX * NY
MESH = pl.DeviceIdType.MESH
F32 = jnp.float32
BF16 = jnp.bfloat16
LN2 = math.log(2.0)

ROWS = 2048
PROT = 1024
DW = 256
TOTAL_ROWS = ROWS * NDP
TOTAL_PROT = PROT * NZ * NC

CH = 256
NCH = ROWS // CH
HALF = ROWS // 2
NB = NZ * NC
PARTS = ((0, 256, "y"), (256, 256, "x"), (512, 256, "x"), (768, 256, "x"))


def split(x):
    hi = x.astype(BF16)
    return hi, (x - hi.astype(F32)).astype(BF16)


def nt(a, b):
    return lax.dot_general(a, b, (((1,), (1,)), ((), ())), preferred_element_type=F32)


def nn(a, b):
    return lax.dot_general(a, b, (((1,), (0,)), ((), ())), preferred_element_type=F32)


def tree(parts, op):
    while len(parts) > 1:
        parts = [op(a, b) for a, b in zip(parts[::2], parts[1::2])]
    return parts[0]


def twice(v):
    return jnp.concatenate([v, v], axis=1)


def fold(v, op):
    return op(v[:, :128], v[:, 128:])


def log_sum(terms):
    peak = tree(terms, jnp.maximum)
    mass = tree([jnp.exp2(t - peak) for t in terms], jnp.add)
    return peak + jnp.log2(mass)


def total(terms):
    return tree(terms, jnp.add)


def kernel(*refs):
    (e_hbm, p_hbm, out, pot_ref, e_ref, p_ref, p3_ref), refs = refs[:7], refs[7:]
    mats, refs = refs[:NCH], refs[NCH:]
    b1s, refs = refs[: len(PARTS)], refs[len(PARTS) :]
    mids, refs = refs[: len(PARTS)], refs[len(PARTS) :]
    b2s, refs = refs[: len(PARTS)], refs[len(PARTS) :]
    (hi_ref, lo_ref, part, wide, peaks, eh2, el2, rb_ref, z_buf, xy_buf, c3x, c3y, sums,
     load_sem, zs, zr, cs, cr, fs, fr, gr) = refs
    dp, bk = lax.axis_index("dp"), lax.axis_index("bucket")
    x, y = lax.div(dp, NY), lax.rem(dp, NY)

    loads_e, loads_p = [], []
    for j in range(NCH):
        rows = pl.ds(CH * j, CH)
        loads_e.append(pltpu.make_async_copy(e_hbm.at[rows], e_ref.at[rows], load_sem.at[j]))
    for q in range(PROT // CH):
        rows = pl.ds(CH * q, CH)
        loads_p.append(pltpu.make_async_copy(p_hbm.at[rows], p_ref.at[rows], load_sem.at[NCH + q]))
    for copy in loads_e[:1] + loads_p + loads_e[1:]:
        copy.start()

    def bk_dev(d):
        return (dp, lax.rem(bk + d, NB))

    def xy_dev(dx, dy):
        return (lax.rem(x + dx, NX) * NY + lax.rem(y + dy, NY), bk)

    xy_peers = sorted(
        [(dx, dy) for dx in range(NX) for dy in range(NY) if dx or dy],
        key=lambda p: -(min(p[0], NX - p[0]) + min(p[1], NY - p[1])),
    )
    bk_peers = sorted(range(1, NB), key=lambda d: -min(d, NB - d))
    x_peers, y_peers = [2, 1, 3], [4, 3, 5, 2, 6, 1, 7]

    barrier = pltpu.get_barrier_semaphore()
    everyone = [bk_dev(d) for d in bk_peers] + [xy_dev(*p) for p in xy_peers]
    for d in everyone:
        pl.semaphore_signal(barrier, 1, device_id=d, device_id_type=MESH)

    def await_bytes(ref, sem):
        pltpu.make_async_copy(ref, ref, sem).wait()

    def send(src, dst, ssem, rsem, device):
        pltpu.make_async_remote_copy(src, dst, ssem, rsem, device_id=device, device_id_type=MESH).start()

    def row_send(n, h, vec):
        z_buf[n, h, bk] = vec
        for d in bk_peers:
            send(z_buf.at[n, h, bk], z_buf.at[n, h, bk], zs.at[2 * n + h], zr.at[2 * n + h], bk_dev(d))

    def row_wait(n, h, combine):
        rest = z_buf.at[n, h, pl.ds(0, NB - 1)]
        await_bytes(rest, zr.at[2 * n + h])
        await_bytes(rest, zs.at[2 * n + h])
        return combine([z_buf[n, h, d] for d in range(NB)])

    def deep(v, op):
        v = op(op(v.reshape(PROT // 32, 4, 8, CH), axis=0), axis=0)
        return op(v, axis=0, keepdims=True)

    lams = []
    for j in range(NCH + 1):
        if j < NCH:
            loads_e[j].wait()
            eh, el = split(e_ref[CH * j : CH * (j + 1), :])
            e3 = jnp.concatenate([eh, el, eh], axis=1)
            for q in range(PROT // CH):
                r = slice(CH * q, CH * (q + 1))
                if j == 0:
                    loads_p[q].wait()
                    ph, plo = split(p_ref[r, :] * F32(2.0 / math.sqrt(DW) / LN2))
                    p3_ref[r, 0:DW] = ph
                    p3_ref[r, DW : 2 * DW] = ph
                    p3_ref[r, 2 * DW :] = plo
                mats[j][r, :] = nt(p3_ref[r, :], e3)
        if j >= 1:
            v = mats[j - 1][...]
            m = deep(v, jnp.max)
            lam = m + jnp.log2(deep(jnp.exp2(v - m), jnp.sum))
            lams += [lam[:, :128], lam[:, 128:]]
        if j == NCH // 2:
            pl.semaphore_wait(barrier, len(everyone))
            row_send(0, 0, jnp.concatenate(lams, axis=0))
            lams = []
    row_send(0, 1, jnp.concatenate(lams, axis=0))

    def col_send(n, vec):
        xy_buf[n, dp] = vec
        for p in xy_peers:
            send(xy_buf.at[n, dp], xy_buf.at[n, dp], cs.at[n], cr.at[n], xy_dev(*p))

    def col_wait(n, combine):
        rest = xy_buf.at[n, pl.ds(0, NDP - 1)]
        await_bytes(rest, cr.at[n])
        await_bytes(rest, cs.at[n])
        return combine([xy_buf[n, d] for d in range(NDP)])

    def to_row(v, reduce):
        return reduce(v.T, axis=0, keepdims=True)

    def to_tile(row):
        return jnp.broadcast_to(row, (128, 128)).T

    def cut(j):
        return slice(CH * j, CH * (j + 1))

    blocks = [slice(128 * a, 128 * (a + 1)) for a in range(PROT // 128)]
    groups = (range(NCH // 2), range(NCH // 2, NCH))

    def half(h):
        return slice(HALF * h, HALF * (h + 1))

    def spread(h, vec):
        for t in range(8):
            rb_ref[:, HALF * h + 128 * t : HALF * h + 128 * (t + 1)] = vec[t : t + 1, :]

    def row_sums(h, vec=None):
        acc = [jnp.zeros((8, CH), F32) for _ in groups[h]]
        for a, r in enumerate(blocks):
            if vec is not None:
                wide[r, :] = to_tile(vec[a : a + 1, :])
            v = twice(wide[r, :])
            acc = [t + jnp.sum((mats[j][r, :] * v).reshape(16, 8, CH), axis=0) for t, j in zip(acc, groups[h])]
        return jnp.concatenate(
            [jnp.sum(t[:, k : k + 128], axis=0, keepdims=True) for t in acc for k in (0, 128)], axis=0)

    def row_step(n, vec):
        row_send(n, 0, row_sums(0, vec))
        row_send(n, 1, row_sums(1))

    def col_terms(r, js):
        return tree([fold(mats[j][r, :] * rb_ref[:, cut(j)], jnp.add) for j in js], jnp.add)

    def peak_terms(r, js):
        return tree([fold(mats[j][r, :] - rb_ref[:, cut(j)], jnp.maximum) for j in js], jnp.maximum)

    spread(0, row_wait(0, 0, log_sum))
    for r in blocks:
        part[r, :] = peak_terms(r, groups[0])
    spread(1, row_wait(0, 1, log_sum))
    rows_of_peaks = []
    for r in blocks:
        row = to_row(jnp.maximum(part[r, :], peak_terms(r, groups[1])), jnp.max)
        rows_of_peaks.append(row)
        peaks[r, :] = to_tile(row)
    peak = jnp.concatenate(rows_of_peaks, axis=0)

    masses = []
    for r in blocks:
        pk = twice(peaks[r, :])
        terms = []
        for j, m in enumerate(mats):
            b = jnp.exp2(m[r, :] - rb_ref[:, cut(j)] - pk)
            m[r, :] = b
            terms.append(fold(b, jnp.add))
        masses.append(to_row(tree(terms, jnp.add), jnp.sum))
    col_send(0, peak + jnp.log2(jnp.concatenate(masses, axis=0)))

    def halves(g, carry):
        r = pl.ds(pl.multiple_of(g * 64, 64), 64)
        for j, m in enumerate(mats):
            h, l = split(m[r, :])
            hi_ref[r, cut(j)] = h
            lo_ref[r, cut(j)] = l
        return carry

    lax.fori_loop(0, PROT // 64, halves, 0)

    g_log = col_wait(0, log_sum)
    w = jnp.exp2(peak - g_log)
    ratio = TOTAL_ROWS / TOTAL_PROT
    row_step(1, w * ratio)
    for a, r in enumerate(blocks):
        peaks[r, :] = to_tile(w[a : a + 1, :])
    spread(0, 1.0 / row_wait(1, 0, total))
    for r in blocks:
        part[r, :] = col_terms(r, groups[0])
    spread(1, 1.0 / row_wait(1, 1, total))
    col_send(1, w * jnp.concatenate([to_row(part[r, :] + col_terms(r, groups[1]), jnp.sum) for r in blocks], axis=0))
    row_step(2, w * ratio / col_wait(1, total))

    def scale_rows(h):
        for a in range(8 * h, 8 * h + 8):
            r = slice(128 * a, 128 * (a + 1))
            t, l = split(e_ref[r, :] * twice(to_tile(rb_ref[:, r])))
            eh2[r, :] = t
            el2[r, :] = l

    def product(r, k):
        h = hi_ref[r, k]
        return nn(h, eh2[k, :]) + nn(h, el2[k, :]) + nn(lo_ref[r, k], eh2[k, :])

    spread(0, 1.0 / row_wait(2, 0, total))
    scale_rows(0)
    first = slice(PARTS[0][0], PARTS[0][0] + PARTS[0][1])
    sums[first, :] = product(first, half(0))
    spread(1, 1.0 / row_wait(2, 1, total))
    scale_rows(1)

    def rows_of(base, unit, index):
        return pl.ds(pl.multiple_of(base + unit * index, 8), unit)

    n_x, n_y = (NX, x, x_peers, lambda d: xy_dev(d, 0)), (NY, y, y_peers, lambda d: xy_dev(0, d))

    def plan(p):
        base, size, first = PARTS[p]
        one, two = (n_x, n_y) if first == "x" else (n_y, n_x)
        return base, size, one, two, size // one[0], size // NDP

    def scatter_one(p):
        base, size, (n, me, peers, dev), _, c1, _ = plan(p)
        for d in peers:
            send(sums.at[rows_of(base, c1, lax.rem(me + d, n))], b1s[p].at[me], fs.at[4 * p], fr.at[4 * p], dev(d))
        b1s[p][me] = sums[rows_of(base, c1, me), :]

    def scatter_two(p):
        _, size, (n1, _, _, _), (n, me, peers, dev), c1, c2 = plan(p)
        await_bytes(b1s[p].at[pl.ds(0, n1 - 1)], fr.at[4 * p])
        mids[p][...] = total([b1s[p][d] for d in range(n1)])
        for d in peers:
            send(mids[p].at[rows_of(0, c2, lax.rem(me + d, n))], b2s[p].at[me], fs.at[4 * p + 1], fr.at[4 * p + 1], dev(d))
        b2s[p][me] = mids[p][rows_of(0, c2, me), :]

    def gather_one(p):
        base, size, (_, me1, _, _), (n, me, peers, dev), c1, c2 = plan(p)
        await_bytes(b2s[p].at[pl.ds(0, n - 1)], fr.at[4 * p + 1])
        own = rows_of(base, c2, me1 * n + me)
        v = total([b2s[p][d] for d in range(n)]) * twice(part[own, :])
        out[own, :] = v * lax.rsqrt(jnp.mean(v * v, axis=1, keepdims=True) + 1e-06)
        for d in peers:
            arrived = fr.at[4 * p + 2] if PARTS[p][2] == "y" else gr.at[NY * p + d]
            send(out.at[own], out.at[own], fs.at[4 * p + 2], arrived, dev(d))
        if PARTS[p][2] == "x":
            for d in x_peers:
                send(out.at[own], out.at[own], fs.at[4 * p + 3], fr.at[4 * p + 3], xy_dev(d, 0))

    def gather_two(p):
        base, size, (_, me, peers, dev), _, c1, c2 = plan(p)
        if PARTS[p][2] == "y":
            await_bytes(out.at[pl.ds(0, c1 - c2)], fr.at[4 * p + 2])
            mid = rows_of(base, c1, me)
            for d in peers:
                send(out.at[mid], out.at[mid], fs.at[4 * p + 3], fr.at[4 * p + 3], dev(d))
            return
        for e in (1, 7, 2, 6, 3, 5, 4):
            got = rows_of(base + c1 * x, c2, lax.rem(y + NY - e, NY))
            await_bytes(out.at[got], gr.at[NY * p + e])
            for d in x_peers:
                send(out.at[got], out.at[got], fs.at[4 * p + 3], fr.at[4 * p + 3], xy_dev(d, 0))

    for p, (base, size, _) in enumerate(PARTS):
        rows = slice(base, base + size)
        acc = sums[rows, :] + product(rows, half(1)) if p == 0 else product(rows, slice(0, ROWS))
        sums[rows, :] = acc * twice(peaks[rows, :])
        scatter_one(p)
        if p == 1:
            c3x[x] = w * jnp.concatenate([to_row(col_terms(r, range(NCH)), jnp.sum) for r in blocks], axis=0)
            for d in x_peers:
                send(c3x.at[x], c3x.at[x], cs.at[2], cr.at[2], xy_dev(d, 0))

    scatter_two(1)
    await_bytes(c3x.at[pl.ds(0, NX - 1)], cr.at[2])
    c3y[y] = total([c3x[d] for d in range(NX)])
    for d in y_peers:
        send(c3y.at[y], c3y.at[y], cs.at[3], cr.at[3], xy_dev(0, d))
    scatter_two(2)
    scatter_two(0)
    scatter_two(3)
    await_bytes(c3y.at[pl.ds(0, NY - 1)], cr.at[3])
    mass = total([c3y[d] for d in range(NY)])
    pot_ref[...] = ((math.log(TOTAL_ROWS / TOTAL_PROT) - LN2 * g_log) - jnp.log(mass)).reshape(pot_ref.shape)
    for a, r in enumerate(blocks):
        part[r, :] = to_tile(1.0 / mass[a : a + 1, :])
    await_bytes(c3x.at[pl.ds(0, NX - 1)], cs.at[2])
    await_bytes(c3y.at[pl.ds(0, NY - 1)], cs.at[3])
    for p in (1, 0, 2, 3):
        gather_one(p)
    for p in (0, 1, 2, 3):
        gather_two(p)
    for p in (0, 1, 2, 3):
        _, size, _, _, c1, c2 = plan(p)
        await_bytes(out.at[pl.ds(0, size - c1)], fr.at[4 * p + 3])
        for n, sent in enumerate((size - c1, c1 - c2, c1 - c2, size - c1)):
            await_bytes(sums.at[pl.ds(0, sent)], fs.at[4 * p + n])


def body(embeddings, prototypes):
    vm = pltpu.VMEM
    dma = pltpu.SemaphoreType.DMA
    counts = [(NX, NY) if first == "x" else (NY, NX) for _, _, first in PARTS]
    sizes = [size for _, size, _ in PARTS]
    new_protos, pot = pl.pallas_call(
        kernel,
        out_shape=(pltpu.VMEM((PROT, DW), F32), pltpu.VMEM((PROT,), F32)),
        in_specs=[pl.BlockSpec(memory_space=pl.ANY)] * 2,
        out_specs=(pl.BlockSpec(memory_space=vm), pl.BlockSpec(memory_space=vm)),
        scratch_shapes=[
            vm((ROWS, DW), F32),
            vm((PROT, DW), F32),
            vm((PROT, 3 * DW), BF16),
            *[vm((PROT, CH), F32) for _ in range(NCH)],
            *[vm((a, s // a, DW), F32) for (a, _), s in zip(counts, sizes)],
            *[vm((s // a, DW), F32) for (a, _), s in zip(counts, sizes)],
            *[vm((b, s // NDP, DW), F32) for (_, b), s in zip(counts, sizes)],
            vm((PROT, ROWS), BF16),
            vm((PROT, ROWS), BF16),
            vm((PROT, 128), F32),
            vm((PROT, 128), F32),
            vm((PROT, 128), F32),
            vm((ROWS, DW), BF16),
            vm((ROWS, DW), BF16),
            vm((1, ROWS), F32),
            vm((3, 2, NB, 8, 128), F32),
            vm((2, NDP, 8, 128), F32),
            vm((NX, 8, 128), F32),
            vm((NY, 8, 128), F32),
            vm((PROT, DW), F32),
            dma((NCH + PROT // CH,)),
            dma((6,)), dma((6,)),
            dma((4,)), dma((4,)),
            dma((4 * len(PARTS),)), dma((4 * len(PARTS),)), dma((NY * len(PARTS),)),
        ],
        compiler_params=pltpu.CompilerParams(
            collective_id=0, has_side_effects=True, vmem_limit_bytes=56 * 1024 * 1024),
        name="sinkhorn",
    )(embeddings, prototypes)
    return new_protos, pot


def solution(mesh):
    in_specs = (P("dp", None), P("bucket", None))
    out_specs = (P("bucket", None), P("bucket"))
    return jax.shard_map(body, mesh=mesh, in_specs=in_specs, out_specs=out_specs, check_vma=False)
```

```python
import math

import jax
import jax.numpy as jnp
from jax import lax
from jax.experimental import pallas as pl
from jax.experimental.pallas import tpu as pltpu
from jax.sharding import PartitionSpec as P

NX, NY, NZ, NC = 4, 8, 8, 2
NDP = NX * NY
MESH = pl.DeviceIdType.MESH
F32 = jnp.float32
BF16 = jnp.bfloat16
LN2 = math.log(2.0)

ROWS = 2048
PROT = 1024
DW = 256
TOTAL_ROWS = ROWS * NDP
TOTAL_PROT = PROT * NZ * NC

CH = 256
NCH = ROWS // CH
HALF = ROWS // 2
NB = NZ * NC
PARTS = ((0, 256, "y"), (256, 256, "x"), (512, 256, "x"), (768, 256, "x"))


def split(x):
    hi = x.astype(BF16)
    return hi, (x - hi.astype(F32)).astype(BF16)


def nt(a, b):
    return lax.dot_general(a, b, (((1,), (1,)), ((), ())), preferred_element_type=F32)


def nn(a, b):
    return lax.dot_general(a, b, (((1,), (0,)), ((), ())), preferred_element_type=F32)


def tree(parts, op):
    while len(parts) > 1:
        parts = [op(a, b) for a, b in zip(parts[::2], parts[1::2])]
    return parts[0]


def twice(v):
    return jnp.concatenate([v, v], axis=1)


def fold(v, op):
    return op(v[:, :128], v[:, 128:])


def log_sum(terms):
    peak = tree(terms, jnp.maximum)
    mass = tree([jnp.exp2(t - peak) for t in terms], jnp.add)
    return peak + jnp.log2(mass)


def total(terms):
    return tree(terms, jnp.add)


def kernel(*refs):
    (e_hbm, p_hbm, out, pot_ref, e_ref, p_ref, p3_ref), refs = refs[:7], refs[7:]
    mats, refs = refs[:NCH], refs[NCH:]
    b1s, refs = refs[: len(PARTS)], refs[len(PARTS) :]
    mids, refs = refs[: len(PARTS)], refs[len(PARTS) :]
    b2s, refs = refs[: len(PARTS)], refs[len(PARTS) :]
    (hi_ref, lo_ref, part, wide, peaks, eh2, el2, rb_ref, z_buf, xy_buf, c3x, c3y, sums,
     load_sem, zs, zr, cs, cr, fs, fr, gr) = refs
    dp, bk = lax.axis_index("dp"), lax.axis_index("bucket")
    x, y = lax.div(dp, NY), lax.rem(dp, NY)

    loads_e, loads_p = [], []
    for j in range(NCH):
        rows = pl.ds(CH * j, CH)
        loads_e.append(pltpu.make_async_copy(e_hbm.at[rows], e_ref.at[rows], load_sem.at[j]))
    for q in range(PROT // CH):
        rows = pl.ds(CH * q, CH)
        loads_p.append(pltpu.make_async_copy(p_hbm.at[rows], p_ref.at[rows], load_sem.at[NCH + q]))
    for copy in loads_e[:1] + loads_p + loads_e[1:]:
        copy.start()

    def bk_dev(d):
        return (dp, lax.rem(bk + d, NB))

    def xy_dev(dx, dy):
        return (lax.rem(x + dx, NX) * NY + lax.rem(y + dy, NY), bk)

    xy_peers = sorted(
        [(dx, dy) for dx in range(NX) for dy in range(NY) if dx or dy],
        key=lambda p: -(min(p[0], NX - p[0]) + min(p[1], NY - p[1])),
    )
    bk_peers = sorted(range(1, NB), key=lambda d: -min(d, NB - d))
    x_peers, y_peers = [2, 1, 3], [4, 3, 5, 2, 6, 1, 7]

    barrier = pltpu.get_barrier_semaphore()
    everyone = [bk_dev(d) for d in bk_peers] + [xy_dev(*p) for p in xy_peers]
    for d in everyone:
        pl.semaphore_signal(barrier, 1, device_id=d, device_id_type=MESH)

    def await_bytes(ref, sem):
        pltpu.make_async_copy(ref, ref, sem).wait()

    def send(src, dst, ssem, rsem, device):
        pltpu.make_async_remote_copy(src, dst, ssem, rsem, device_id=device, device_id_type=MESH).start()

    def row_send(n, h, vec):
        z_buf[n, h, bk] = vec
        for d in bk_peers:
            send(z_buf.at[n, h, bk], z_buf.at[n, h, bk], zs.at[2 * n + h], zr.at[2 * n + h], bk_dev(d))

    def row_wait(n, h, combine):
        rest = z_buf.at[n, h, pl.ds(0, NB - 1)]
        await_bytes(rest, zr.at[2 * n + h])
        return combine([z_buf[n, h, d] for d in range(NB)])

    def deep(v, op):
        v = op(op(v.reshape(PROT // 32, 4, 8, CH), axis=0), axis=0)
        return op(v, axis=0, keepdims=True)

    lams = []
    for j in range(NCH + 1):
        if j < NCH:
            loads_e[j].wait()
            eh, el = split(e_ref[CH * j : CH * (j + 1), :])
            e3 = jnp.concatenate([eh, el, eh], axis=1)
            for q in range(PROT // CH):
                r = slice(CH * q, CH * (q + 1))
                if j == 0:
                    loads_p[q].wait()
                    ph, plo = split(p_ref[r, :] * F32(2.0 / math.sqrt(DW) / LN2))
                    p3_ref[r, 0:DW] = ph
                    p3_ref[r, DW : 2 * DW] = ph
                    p3_ref[r, 2 * DW :] = plo
                mats[j][r, :] = nt(p3_ref[r, :], e3)
        if j >= 1:
            v = mats[j - 1][...]
            m = deep(v, jnp.max)
            lam = m + jnp.log2(deep(jnp.exp2(v - m), jnp.sum))
            lams += [lam[:, :128], lam[:, 128:]]
        if j == NCH // 2:
            pl.semaphore_wait(barrier, len(everyone))
            row_send(0, 0, jnp.concatenate(lams, axis=0))
            lams = []
    row_send(0, 1, jnp.concatenate(lams, axis=0))

    def col_send(n, vec):
        xy_buf[n, dp] = vec
        for p in xy_peers:
            send(xy_buf.at[n, dp], xy_buf.at[n, dp], cs.at[n], cr.at[n], xy_dev(*p))

    def col_wait(n, combine):
        rest = xy_buf.at[n, pl.ds(0, NDP - 1)]
        await_bytes(rest, cr.at[n])
        return combine([xy_buf[n, d] for d in range(NDP)])

    def to_row(v, reduce):
        return reduce(v.T, axis=0, keepdims=True)

    def to_tile(row):
        return jnp.broadcast_to(row, (128, 128)).T

    def cut(j):
        return slice(CH * j, CH * (j + 1))

    blocks = [slice(128 * a, 128 * (a + 1)) for a in range(PROT // 128)]
    groups = (range(NCH // 2), range(NCH // 2, NCH))

    def half(h):
        return slice(HALF * h, HALF * (h + 1))

    def spread(h, vec):
        for t in range(8):
            rb_ref[:, HALF * h + 128 * t : HALF * h + 128 * (t + 1)] = vec[t : t + 1, :]

    def row_sums(h, vec=None):
        acc = [jnp.zeros((8, CH), F32) for _ in groups[h]]
        for a, r in enumerate(blocks):
            if vec is not None:
                wide[r, :] = to_tile(vec[a : a + 1, :])
            v = twice(wide[r, :])
            acc = [t + jnp.sum((mats[j][r, :] * v).reshape(16, 8, CH), axis=0) for t, j in zip(acc, groups[h])]
        return jnp.concatenate(
            [jnp.sum(t[:, k : k + 128], axis=0, keepdims=True) for t in acc for k in (0, 128)], axis=0)

    def row_step(n, vec):
        row_send(n, 0, row_sums(0, vec))
        row_send(n, 1, row_sums(1))

    def col_terms(r, js):
        return tree([fold(mats[j][r, :] * rb_ref[:, cut(j)], jnp.add) for j in js], jnp.add)

    def peak_terms(r, js):
        return tree([fold(mats[j][r, :] - rb_ref[:, cut(j)], jnp.maximum) for j in js], jnp.maximum)

    spread(0, row_wait(0, 0, log_sum))
    for r in blocks:
        part[r, :] = peak_terms(r, groups[0])
    spread(1, row_wait(0, 1, log_sum))
    rows_of_peaks = []
    for r in blocks:
        row = to_row(jnp.maximum(part[r, :], peak_terms(r, groups[1])), jnp.max)
        rows_of_peaks.append(row)
        peaks[r, :] = to_tile(row)
    peak = jnp.concatenate(rows_of_peaks, axis=0)

    masses = []
    for r in blocks:
        pk = twice(peaks[r, :])
        terms = []
        for j, m in enumerate(mats):
            b = jnp.exp2(m[r, :] - rb_ref[:, cut(j)] - pk)
            m[r, :] = b
            terms.append(fold(b, jnp.add))
        masses.append(to_row(tree(terms, jnp.add), jnp.sum))
    col_send(0, peak + jnp.log2(jnp.concatenate(masses, axis=0)))

    def halves(g, carry):
        r = pl.ds(pl.multiple_of(g * 64, 64), 64)
        for j, m in enumerate(mats):
            h, l = split(m[r, :])
            hi_ref[r, cut(j)] = h
            lo_ref[r, cut(j)] = l
        return carry

    lax.fori_loop(0, PROT // 64, halves, 0)

    g_log = col_wait(0, log_sum)
    w = jnp.exp2(peak - g_log)
    ratio = TOTAL_ROWS / TOTAL_PROT
    row_step(1, w * ratio)
    for a, r in enumerate(blocks):
        peaks[r, :] = to_tile(w[a : a + 1, :])
    spread(0, 1.0 / row_wait(1, 0, total))
    for r in blocks:
        part[r, :] = col_terms(r, groups[0])
    spread(1, 1.0 / row_wait(1, 1, total))
    col_send(1, w * jnp.concatenate([to_row(part[r, :] + col_terms(r, groups[1]), jnp.sum) for r in blocks], axis=0))
    row_step(2, w * ratio / col_wait(1, total))

    def scale_rows(h):
        for a in range(8 * h, 8 * h + 8):
            r = slice(128 * a, 128 * (a + 1))
            t, l = split(e_ref[r, :] * twice(to_tile(rb_ref[:, r])))
            eh2[r, :] = t
            el2[r, :] = l

    def product(r, k):
        h = hi_ref[r, k]
        return nn(h, eh2[k, :]) + nn(h, el2[k, :]) + nn(lo_ref[r, k], eh2[k, :])

    spread(0, 1.0 / row_wait(2, 0, total))
    scale_rows(0)
    first = slice(PARTS[0][0], PARTS[0][0] + PARTS[0][1])
    sums[first, :] = product(first, half(0))
    spread(1, 1.0 / row_wait(2, 1, total))
    scale_rows(1)

    def rows_of(base, unit, index):
        return pl.ds(pl.multiple_of(base + unit * index, 8), unit)

    n_x, n_y = (NX, x, x_peers, lambda d: xy_dev(d, 0)), (NY, y, y_peers, lambda d: xy_dev(0, d))

    def plan(p):
        base, size, first = PARTS[p]
        one, two = (n_x, n_y) if first == "x" else (n_y, n_x)
        return base, size, one, two, size // one[0], size // NDP

    def scatter_one(p):
        base, size, (n, me, peers, dev), _, c1, _ = plan(p)
        for d in peers:
            send(sums.at[rows_of(base, c1, lax.rem(me + d, n))], b1s[p].at[me], fs.at[4 * p], fr.at[4 * p], dev(d))
        b1s[p][me] = sums[rows_of(base, c1, me), :]

    def scatter_two(p):
        _, size, (n1, _, _, _), (n, me, peers, dev), c1, c2 = plan(p)
        await_bytes(b1s[p].at[pl.ds(0, n1 - 1)], fr.at[4 * p])
        mids[p][...] = total([b1s[p][d] for d in range(n1)])
        for d in peers:
            send(mids[p].at[rows_of(0, c2, lax.rem(me + d, n))], b2s[p].at[me], fs.at[4 * p + 1], fr.at[4 * p + 1], dev(d))
        b2s[p][me] = mids[p][rows_of(0, c2, me), :]

    def gather_one(p):
        base, size, (_, me1, _, _), (n, me, peers, dev), c1, c2 = plan(p)
        await_bytes(b2s[p].at[pl.ds(0, n - 1)], fr.at[4 * p + 1])
        own = rows_of(base, c2, me1 * n + me)
        v = total([b2s[p][d] for d in range(n)]) * twice(part[own, :])
        out[own, :] = v * lax.rsqrt(jnp.mean(v * v, axis=1, keepdims=True) + 1e-06)
        for d in peers:
            arrived = fr.at[4 * p + 2] if PARTS[p][2] == "y" else gr.at[NY * p + d]
            send(out.at[own], out.at[own], fs.at[4 * p + 2], arrived, dev(d))
        if PARTS[p][2] == "x":
            for d in x_peers:
                send(out.at[own], out.at[own], fs.at[4 * p + 3], fr.at[4 * p + 3], xy_dev(d, 0))

    def gather_two(p):
        base, size, (_, me, peers, dev), _, c1, c2 = plan(p)
        if PARTS[p][2] == "y":
            await_bytes(out.at[pl.ds(0, c1 - c2)], fr.at[4 * p + 2])
            mid = rows_of(base, c1, me)
            for d in peers:
                send(out.at[mid], out.at[mid], fs.at[4 * p + 3], fr.at[4 * p + 3], dev(d))
            return
        for e in (1, 7, 2, 6, 3, 5, 4):
            got = rows_of(base + c1 * x, c2, lax.rem(y + NY - e, NY))
            await_bytes(out.at[got], gr.at[NY * p + e])
            for d in x_peers:
                send(out.at[got], out.at[got], fs.at[4 * p + 3], fr.at[4 * p + 3], xy_dev(d, 0))

    for p, (base, size, _) in enumerate(PARTS):
        rows = slice(base, base + size)
        acc = sums[rows, :] + product(rows, half(1)) if p == 0 else product(rows, slice(0, ROWS))
        sums[rows, :] = acc * twice(peaks[rows, :])
        scatter_one(p)
        if p == 1:
            c3x[x] = w * jnp.concatenate([to_row(col_terms(r, range(NCH)), jnp.sum) for r in blocks], axis=0)
            for d in x_peers:
                send(c3x.at[x], c3x.at[x], cs.at[2], cr.at[2], xy_dev(d, 0))

    scatter_two(1)
    await_bytes(c3x.at[pl.ds(0, NX - 1)], cr.at[2])
    c3y[y] = total([c3x[d] for d in range(NX)])
    for d in y_peers:
        send(c3y.at[y], c3y.at[y], cs.at[3], cr.at[3], xy_dev(0, d))
    scatter_two(2)
    scatter_two(0)
    scatter_two(3)
    await_bytes(c3y.at[pl.ds(0, NY - 1)], cr.at[3])
    mass = total([c3y[d] for d in range(NY)])
    pot_ref[...] = ((math.log(TOTAL_ROWS / TOTAL_PROT) - LN2 * g_log) - jnp.log(mass)).reshape(pot_ref.shape)
    for a, r in enumerate(blocks):
        part[r, :] = to_tile(1.0 / mass[a : a + 1, :])
    for p in (1, 0, 2, 3):
        gather_one(p)
    for p in (0, 1, 2, 3):
        gather_two(p)
    for p in (0, 1, 2, 3):
        _, size, _, _, c1, c2 = plan(p)
        await_bytes(out.at[pl.ds(0, size - c1)], fr.at[4 * p + 3])
        for n, sent in enumerate((size - c1, c1 - c2, c1 - c2, size - c1)):
            await_bytes(sums.at[pl.ds(0, sent)], fs.at[4 * p + n])

    for n in range(2):
        await_bytes(xy_buf.at[n, pl.ds(0, NDP - 1)], cs.at[n])
    for n in range(6):
        await_bytes(z_buf.at[n // 2, n % 2, pl.ds(0, NB - 1)], zs.at[n])
    await_bytes(c3x.at[pl.ds(0, NX - 1)], cs.at[2])
    await_bytes(c3y.at[pl.ds(0, NY - 1)], cs.at[3])


def store(a, b, a_out, b_out, sems):
    copies = [pltpu.make_async_copy(a, a_out, sems.at[0]), pltpu.make_async_copy(b, b_out, sems.at[1])]
    for copy in copies:
        copy.start()
    for copy in copies:
        copy.wait()


def body(embeddings, prototypes):
    vm = pltpu.VMEM
    dma = pltpu.SemaphoreType.DMA
    counts = [(NX, NY) if first == "x" else (NY, NX) for _, _, first in PARTS]
    sizes = [size for _, size, _ in PARTS]
    new_protos, pot = pl.pallas_call(
        kernel,
        out_shape=(pltpu.VMEM((PROT, DW), F32), pltpu.VMEM((PROT,), F32)),
        in_specs=[pl.BlockSpec(memory_space=pl.ANY)] * 2,
        out_specs=(pl.BlockSpec(memory_space=vm), pl.BlockSpec(memory_space=vm)),
        scratch_shapes=[
            vm((ROWS, DW), F32),
            vm((PROT, DW), F32),
            vm((PROT, 3 * DW), BF16),
            *[vm((PROT, CH), F32) for _ in range(NCH)],
            *[vm((a, s // a, DW), F32) for (a, _), s in zip(counts, sizes)],
            *[vm((s // a, DW), F32) for (a, _), s in zip(counts, sizes)],
            *[vm((b, s // NDP, DW), F32) for (_, b), s in zip(counts, sizes)],
            vm((PROT, ROWS), BF16),
            vm((PROT, ROWS), BF16),
            vm((PROT, 128), F32),
            vm((PROT, 128), F32),
            vm((PROT, 128), F32),
            vm((ROWS, DW), BF16),
            vm((ROWS, DW), BF16),
            vm((1, ROWS), F32),
            vm((3, 2, NB, 8, 128), F32),
            vm((2, NDP, 8, 128), F32),
            vm((NX, 8, 128), F32),
            vm((NY, 8, 128), F32),
            vm((PROT, DW), F32),
            dma((NCH + PROT // CH,)),
            dma((6,)), dma((6,)),
            dma((4,)), dma((4,)),
            dma((4 * len(PARTS),)), dma((4 * len(PARTS),)), dma((NY * len(PARTS),)),
        ],
        compiler_params=pltpu.CompilerParams(
            collective_id=0, has_side_effects=True, vmem_limit_bytes=56 * 1024 * 1024),
        name="sinkhorn",
    )(embeddings, prototypes)
    return pl.pallas_call(
        store,
        out_shape=(jax.ShapeDtypeStruct((PROT, DW), F32), jax.ShapeDtypeStruct((PROT,), F32)),
        in_specs=[pl.BlockSpec(memory_space=pl.ANY)] * 2,
        out_specs=(pl.BlockSpec(memory_space=pl.ANY), pl.BlockSpec(memory_space=pl.ANY)),
        scratch_shapes=[dma((2,))],
        name="store",
    )(new_protos, pot)


def solution(mesh):
    in_specs = (P("dp", None), P("bucket", None))
    out_specs = (P("bucket", None), P("bucket"))
    return jax.shard_map(body, mesh=mesh, in_specs=in_specs, out_specs=out_specs, check_vma=False)
```

```python
import math

import jax
import jax.numpy as jnp
from jax import lax
from jax.experimental import pallas as pl
from jax.experimental.pallas import tpu as pltpu
from jax.sharding import PartitionSpec as P

NX, NY, NZ, NC = 4, 8, 8, 2
NDP = NX * NY
MESH = pl.DeviceIdType.MESH
F32 = jnp.float32
BF16 = jnp.bfloat16
LN2 = math.log(2.0)

ROWS = 2048
PROT = 1024
DW = 256
TOTAL_ROWS = ROWS * NDP
TOTAL_PROT = PROT * NZ * NC

CH = 256
NCH = ROWS // CH
HALF = ROWS // 2
NB = NZ * NC
PARTS = ((0, 256, "y"), (256, 256, "x"), (512, 256, "x"), (768, 256, "x"))


def split(x):
    hi = x.astype(BF16)
    return hi, (x - hi.astype(F32)).astype(BF16)


def nt(a, b):
    return lax.dot_general(a, b, (((1,), (1,)), ((), ())), preferred_element_type=F32)


def nn(a, b):
    return lax.dot_general(a, b, (((1,), (0,)), ((), ())), preferred_element_type=F32)


def tree(parts, op):
    while len(parts) > 1:
        parts = [op(a, b) for a, b in zip(parts[::2], parts[1::2])]
    return parts[0]


def twice(v):
    return jnp.concatenate([v, v], axis=1)


def fold(v, op):
    return op(v[:, :128], v[:, 128:])


def log_sum(terms):
    peak = tree(terms, jnp.maximum)
    mass = tree([jnp.exp2(t - peak) for t in terms], jnp.add)
    return peak + jnp.log2(mass)


def total(terms):
    return tree(terms, jnp.add)


def kernel(*refs):
    (e_hbm, p_hbm, out, pot_ref, e_ref, p_ref, p3_ref), refs = refs[:7], refs[7:]
    mats, refs = refs[:NCH], refs[NCH:]
    b1s, refs = refs[: len(PARTS)], refs[len(PARTS) :]
    mids, refs = refs[: len(PARTS)], refs[len(PARTS) :]
    b2s, refs = refs[: len(PARTS)], refs[len(PARTS) :]
    (hi_ref, lo_ref, part, wide, peaks, eh2, el2, rb_ref, z_buf, xy_buf, c3x, c3y, sums,
     load_sem, zs, zr, cs, cr, fs, fr, gr) = refs
    dp, bk = lax.axis_index("dp"), lax.axis_index("bucket")
    x, y = lax.div(dp, NY), lax.rem(dp, NY)

    loads_e, loads_p = [], []
    for j in range(NCH):
        rows = pl.ds(CH * j, CH)
        loads_e.append(pltpu.make_async_copy(e_hbm.at[rows], e_ref.at[rows], load_sem.at[j]))
    for q in range(PROT // CH):
        rows = pl.ds(CH * q, CH)
        loads_p.append(pltpu.make_async_copy(p_hbm.at[rows], p_ref.at[rows], load_sem.at[NCH + q]))
    for copy in loads_e[:1] + loads_p + loads_e[1:]:
        copy.start()

    def bk_dev(d):
        return (dp, lax.rem(bk + d, NB))

    def xy_dev(dx, dy):
        return (lax.rem(x + dx, NX) * NY + lax.rem(y + dy, NY), bk)

    xy_peers = sorted(
        [(dx, dy) for dx in range(NX) for dy in range(NY) if dx or dy],
        key=lambda p: -(min(p[0], NX - p[0]) + min(p[1], NY - p[1])),
    )
    bk_peers = sorted(range(1, NB), key=lambda d: -min(d, NB - d))
    x_peers, y_peers = [2, 1, 3], [4, 3, 5, 2, 6, 1, 7]

    barrier = pltpu.get_barrier_semaphore()
    everyone = [bk_dev(d) for d in bk_peers] + [xy_dev(*p) for p in xy_peers]
    for d in everyone:
        pl.semaphore_signal(barrier, 1, device_id=d, device_id_type=MESH)

    def await_bytes(ref, sem):
        pltpu.make_async_copy(ref, ref, sem).wait()

    def send(src, dst, ssem, rsem, device):
        pltpu.make_async_remote_copy(src, dst, ssem, rsem, device_id=device, device_id_type=MESH).start()

    def row_send(n, h, vec):
        z_buf[n, h, bk] = vec
        for d in bk_peers:
            send(z_buf.at[n, h, bk], z_buf.at[n, h, bk], zs.at[2 * n + h], zr.at[2 * n + h], bk_dev(d))

    def row_wait(n, h, combine):
        rest = z_buf.at[n, h, pl.ds(0, NB - 1)]
        await_bytes(rest, zr.at[2 * n + h])
        return combine([z_buf[n, h, d] for d in range(NB)])

    def deep(v, op):
        v = op(op(v.reshape(PROT // 32, 4, 8, CH), axis=0), axis=0)
        return op(v, axis=0, keepdims=True)

    lams = []
    for j in range(NCH + 1):
        if j < NCH:
            loads_e[j].wait()
            eh, el = split(e_ref[CH * j : CH * (j + 1), :])
            e3 = jnp.concatenate([eh, el, eh], axis=1)
            for q in range(PROT // CH):
                r = slice(CH * q, CH * (q + 1))
                if j == 0:
                    loads_p[q].wait()
                    ph, plo = split(p_ref[r, :] * F32(2.0 / math.sqrt(DW) / LN2))
                    p3_ref[r, 0:DW] = ph
                    p3_ref[r, DW : 2 * DW] = ph
                    p3_ref[r, 2 * DW :] = plo
                mats[j][r, :] = nt(p3_ref[r, :], e3)
        if j >= 1:
            v = mats[j - 1][...]
            m = deep(v, jnp.max)
            lam = m + jnp.log2(deep(jnp.exp2(v - m), jnp.sum))
            lams += [lam[:, :128], lam[:, 128:]]
        if j == NCH // 2:
            pl.semaphore_wait(barrier, len(everyone))
            row_send(0, 0, jnp.concatenate(lams, axis=0))
            lams = []
    row_send(0, 1, jnp.concatenate(lams, axis=0))

    def col_send(n, h, rows):
        xy_buf[n, h, dp] = jnp.concatenate(rows, axis=0)
        for p in xy_peers:
            send(xy_buf.at[n, h, dp], xy_buf.at[n, h, dp], cs.at[2 * n + h], cr.at[2 * n + h], xy_dev(*p))

    def col_wait(n, h, combine):
        await_bytes(xy_buf.at[n, h, pl.ds(0, NDP - 1)], cr.at[2 * n + h])
        return combine([xy_buf[n, h, d] for d in range(NDP)])

    def to_row(v, reduce):
        return reduce(v.T, axis=0, keepdims=True)

    def to_tile(row):
        return jnp.broadcast_to(row, (128, 128)).T

    def cut(j):
        return slice(CH * j, CH * (j + 1))

    blocks = [slice(128 * a, 128 * (a + 1)) for a in range(PROT // 128)]
    groups = (range(NCH // 2), range(NCH // 2, NCH))

    def half(h):
        return slice(HALF * h, HALF * (h + 1))

    def spread(h, vec):
        for t in range(8):
            rb_ref[:, HALF * h + 128 * t : HALF * h + 128 * (t + 1)] = vec[t : t + 1, :]

    def row_sums(acc, js, h):
        for r in blocks[4 * h : 4 * h + 4]:
            v = twice(wide[r, :])
            for j in js:
                acc[j] = acc[j] + jnp.sum((mats[j][r, :] * v).reshape(16, 8, CH), axis=0)

    def row_step(n, column):
        acc = [jnp.zeros((8, CH), F32) for _ in mats]
        for h in (0, 1):
            v = column(h)
            for a in range(4):
                wide[blocks[4 * h + a], :] = to_tile(v[a : a + 1, :])
            if h == 0:
                row_sums(acc, range(NCH), 0)
        for h in (0, 1):
            row_sums(acc, groups[h], 1)
            row_send(n, h, jnp.concatenate(
                [jnp.sum(acc[j][:, k : k + 128], axis=0, keepdims=True) for j in groups[h] for k in (0, 128)], axis=0))

    def col_terms(r, js):
        return tree([fold(mats[j][r, :] * rb_ref[:, cut(j)], jnp.add) for j in js], jnp.add)

    def peak_terms(r, js):
        return tree([fold(mats[j][r, :] - rb_ref[:, cut(j)], jnp.maximum) for j in js], jnp.maximum)

    spread(0, row_wait(0, 0, log_sum))
    for r in blocks:
        part[r, :] = peak_terms(r, groups[0])
    spread(1, row_wait(0, 1, log_sum))
    rows_of_peaks = []
    for r in blocks:
        row = to_row(jnp.maximum(part[r, :], peak_terms(r, groups[1])), jnp.max)
        rows_of_peaks.append(row)
        peaks[r, :] = to_tile(row)
    peak = [jnp.concatenate(rows_of_peaks[4 * h : 4 * h + 4], axis=0) for h in (0, 1)]

    masses = []
    for n, r in enumerate(blocks):
        pk = twice(peaks[r, :])
        terms = []
        for j, m in enumerate(mats):
            b = jnp.exp2(m[r, :] - rb_ref[:, cut(j)] - pk)
            m[r, :] = b
            terms.append(fold(b, jnp.add))
        masses.append(rows_of_peaks[n] + jnp.log2(to_row(tree(terms, jnp.add), jnp.sum)))
        if n % 4 == 3:
            col_send(0, n // 4, masses[-4:])

    def halves(g, carry):
        r = pl.ds(pl.multiple_of(g * 64, 64), 64)
        for j, m in enumerate(mats):
            h, l = split(m[r, :])
            hi_ref[r, cut(j)] = h
            lo_ref[r, cut(j)] = l
        return carry

    lax.fori_loop(0, PROT // 64, halves, 0)

    ratio = TOTAL_ROWS / TOTAL_PROT
    g_log, w = [], []

    def first_column(h):
        g_log.append(col_wait(0, h, log_sum))
        w.append(jnp.exp2(peak[h] - g_log[h]))
        return w[h] * ratio

    row_step(1, first_column)
    for a, r in enumerate(blocks):
        peaks[r, :] = to_tile(w[a // 4][a % 4 : a % 4 + 1, :])
    spread(0, 1.0 / row_wait(1, 0, total))
    for r in blocks:
        part[r, :] = col_terms(r, groups[0])
    spread(1, 1.0 / row_wait(1, 1, total))
    for h in (0, 1):
        rows = [to_row(part[r, :] + col_terms(r, groups[1]), jnp.sum) for r in blocks[4 * h : 4 * h + 4]]
        col_send(1, h, [w[h][a : a + 1, :] * row for a, row in enumerate(rows)])
    row_step(2, lambda h: w[h] * ratio / col_wait(1, h, total))
    w, g_log = jnp.concatenate(w, axis=0), jnp.concatenate(g_log, axis=0)

    def scale_rows(h):
        for a in range(8 * h, 8 * h + 8):
            r = slice(128 * a, 128 * (a + 1))
            t, l = split(e_ref[r, :] * twice(to_tile(rb_ref[:, r])))
            eh2[r, :] = t
            el2[r, :] = l

    def product(r, k):
        h = hi_ref[r, k]
        return nn(h, eh2[k, :]) + nn(h, el2[k, :]) + nn(lo_ref[r, k], eh2[k, :])

    spread(0, 1.0 / row_wait(2, 0, total))
    scale_rows(0)
    first = slice(PARTS[0][0], PARTS[0][0] + PARTS[0][1])
    sums[first, :] = product(first, half(0))
    spread(1, 1.0 / row_wait(2, 1, total))
    scale_rows(1)

    def rows_of(base, unit, index):
        return pl.ds(pl.multiple_of(base + unit * index, 8), unit)

    n_x, n_y = (NX, x, x_peers, lambda d: xy_dev(d, 0)), (NY, y, y_peers, lambda d: xy_dev(0, d))

    def plan(p):
        base, size, first = PARTS[p]
        one, two = (n_x, n_y) if first == "x" else (n_y, n_x)
        return base, size, one, two, size // one[0], size // NDP

    def scatter_one(p):
        base, size, (n, me, peers, dev), _, c1, _ = plan(p)
        for d in peers:
            send(sums.at[rows_of(base, c1, lax.rem(me + d, n))], b1s[p].at[me], fs.at[4 * p], fr.at[4 * p], dev(d))
        b1s[p][me] = sums[rows_of(base, c1, me), :]

    def scatter_two(p):
        _, size, (n1, _, _, _), (n, me, peers, dev), c1, c2 = plan(p)
        await_bytes(b1s[p].at[pl.ds(0, n1 - 1)], fr.at[4 * p])
        mids[p][...] = total([b1s[p][d] for d in range(n1)])
        for d in peers:
            send(mids[p].at[rows_of(0, c2, lax.rem(me + d, n))], b2s[p].at[me], fs.at[4 * p + 1], fr.at[4 * p + 1], dev(d))
        b2s[p][me] = mids[p][rows_of(0, c2, me), :]

    def gather_one(p):
        base, size, (_, me1, _, _), (n, me, peers, dev), c1, c2 = plan(p)
        await_bytes(b2s[p].at[pl.ds(0, n - 1)], fr.at[4 * p + 1])
        own = rows_of(base, c2, me1 * n + me)
        v = total([b2s[p][d] for d in range(n)]) * twice(part[own, :])
        out[own, :] = v * lax.rsqrt(jnp.mean(v * v, axis=1, keepdims=True) + 1e-06)
        for d in peers:
            arrived = fr.at[4 * p + 2] if PARTS[p][2] == "y" else gr.at[NY * p + d]
            send(out.at[own], out.at[own], fs.at[4 * p + 2], arrived, dev(d))
        if PARTS[p][2] == "x":
            for d in x_peers:
                send(out.at[own], out.at[own], fs.at[4 * p + 3], fr.at[4 * p + 3], xy_dev(d, 0))

    def gather_two(p):
        base, size, (_, me, peers, dev), _, c1, c2 = plan(p)
        if PARTS[p][2] == "y":
            await_bytes(out.at[pl.ds(0, c1 - c2)], fr.at[4 * p + 2])
            mid = rows_of(base, c1, me)
            for d in peers:
                send(out.at[mid], out.at[mid], fs.at[4 * p + 3], fr.at[4 * p + 3], dev(d))
            return
        for e in (1, 7, 2, 6, 3, 5, 4):
            got = rows_of(base + c1 * x, c2, lax.rem(y + NY - e, NY))
            await_bytes(out.at[got], gr.at[NY * p + e])
            for d in x_peers:
                send(out.at[got], out.at[got], fs.at[4 * p + 3], fr.at[4 * p + 3], xy_dev(d, 0))

    for p, (base, size, _) in enumerate(PARTS):
        rows = slice(base, base + size)
        acc = sums[rows, :] + product(rows, half(1)) if p == 0 else product(rows, slice(0, ROWS))
        sums[rows, :] = acc * twice(peaks[rows, :])
        scatter_one(p)
        if p == 1:
            c3x[x] = w * jnp.concatenate([to_row(col_terms(r, range(NCH)), jnp.sum) for r in blocks], axis=0)
            for d in x_peers:
                send(c3x.at[x], c3x.at[x], cs.at[4], cr.at[4], xy_dev(d, 0))

    scatter_two(1)
    await_bytes(c3x.at[pl.ds(0, NX - 1)], cr.at[4])
    c3y[y] = total([c3x[d] for d in range(NX)])
    for d in y_peers:
        send(c3y.at[y], c3y.at[y], cs.at[5], cr.at[5], xy_dev(0, d))
    scatter_two(2)
    scatter_two(0)
    scatter_two(3)
    await_bytes(c3y.at[pl.ds(0, NY - 1)], cr.at[5])
    mass = total([c3y[d] for d in range(NY)])
    pot_ref[...] = ((math.log(TOTAL_ROWS / TOTAL_PROT) - LN2 * g_log) - jnp.log(mass)).reshape(pot_ref.shape)
    for a, r in enumerate(blocks):
        part[r, :] = to_tile(1.0 / mass[a : a + 1, :])
    for p in (1, 0, 2, 3):
        gather_one(p)
    for p in (0, 1, 2, 3):
        gather_two(p)
    for p in (0, 1, 2, 3):
        _, size, _, _, c1, c2 = plan(p)
        await_bytes(out.at[pl.ds(0, size - c1)], fr.at[4 * p + 3])
        for n, sent in enumerate((size - c1, c1 - c2, c1 - c2, size - c1)):
            await_bytes(sums.at[pl.ds(0, sent)], fs.at[4 * p + n])

    for n in range(4):
        await_bytes(xy_buf.at[n // 2, n % 2, pl.ds(0, NDP - 1)], cs.at[n])
    for n in range(6):
        await_bytes(z_buf.at[n // 2, n % 2, pl.ds(0, NB - 1)], zs.at[n])
    await_bytes(c3x.at[pl.ds(0, NX - 1)], cs.at[4])
    await_bytes(c3y.at[pl.ds(0, NY - 1)], cs.at[5])


def body(embeddings, prototypes):
    vm = pltpu.VMEM
    dma = pltpu.SemaphoreType.DMA
    counts = [(NX, NY) if first == "x" else (NY, NX) for _, _, first in PARTS]
    sizes = [size for _, size, _ in PARTS]
    new_protos, pot = pl.pallas_call(
        kernel,
        out_shape=(pltpu.VMEM((PROT, DW), F32), pltpu.VMEM((PROT,), F32)),
        in_specs=[pl.BlockSpec(memory_space=pl.ANY)] * 2,
        out_specs=(pl.BlockSpec(memory_space=vm), pl.BlockSpec(memory_space=vm)),
        scratch_shapes=[
            vm((ROWS, DW), F32),
            vm((PROT, DW), F32),
            vm((PROT, 3 * DW), BF16),
            *[vm((PROT, CH), F32) for _ in range(NCH)],
            *[vm((a, s // a, DW), F32) for (a, _), s in zip(counts, sizes)],
            *[vm((s // a, DW), F32) for (a, _), s in zip(counts, sizes)],
            *[vm((b, s // NDP, DW), F32) for (_, b), s in zip(counts, sizes)],
            vm((PROT, ROWS), BF16),
            vm((PROT, ROWS), BF16),
            vm((PROT, 128), F32),
            vm((PROT, 128), F32),
            vm((PROT, 128), F32),
            vm((ROWS, DW), BF16),
            vm((ROWS, DW), BF16),
            vm((1, ROWS), F32),
            vm((3, 2, NB, 8, 128), F32),
            vm((2, 2, NDP, 4, 128), F32),
            vm((NX, 8, 128), F32),
            vm((NY, 8, 128), F32),
            vm((PROT, DW), F32),
            dma((NCH + PROT // CH,)),
            dma((6,)), dma((6,)),
            dma((6,)), dma((6,)),
            dma((4 * len(PARTS),)), dma((4 * len(PARTS),)), dma((NY * len(PARTS),)),
        ],
        compiler_params=pltpu.CompilerParams(
            collective_id=0, has_side_effects=True, vmem_limit_bytes=56 * 1024 * 1024),
        name="sinkhorn",
    )(embeddings, prototypes)
    return new_protos, pot


def solution(mesh):
    in_specs = (P("dp", None), P("bucket", None))
    out_specs = (P("bucket", None), P("bucket"))
    return jax.shard_map(body, mesh=mesh, in_specs=in_specs, out_specs=out_specs, check_vma=False)
```

```python
import math

import jax
import jax.numpy as jnp
from jax import lax
from jax.experimental import pallas as pl
from jax.experimental.pallas import tpu as pltpu
from jax.sharding import PartitionSpec as P

NX, NY, NZ, NC = 4, 8, 8, 2
NDP = NX * NY
MESH = pl.DeviceIdType.MESH
F32 = jnp.float32
BF16 = jnp.bfloat16
LN2 = math.log(2.0)

ROWS = 2048
PROT = 1024
DW = 256
TOTAL_ROWS = ROWS * NDP
TOTAL_PROT = PROT * NZ * NC

CH = 256
NCH = ROWS // CH
HALF = ROWS // 2
NB = NZ * NC
PARTS = ((0, 256, "y"), (256, 256, "x"), (512, 256, "x"), (768, 256, "x"))


def split(x):
    hi = x.astype(BF16)
    return hi, (x - hi.astype(F32)).astype(BF16)


def nt(a, b):
    return lax.dot_general(a, b, (((1,), (1,)), ((), ())), preferred_element_type=F32)


def nn(a, b):
    return lax.dot_general(a, b, (((1,), (0,)), ((), ())), preferred_element_type=F32)


def tree(parts, op):
    while len(parts) > 1:
        parts = [op(a, b) for a, b in zip(parts[::2], parts[1::2])]
    return parts[0]


def twice(v):
    return jnp.concatenate([v, v], axis=1)


def fold(v, op):
    return op(v[:, :128], v[:, 128:])


def log_sum(terms):
    peak = tree(terms, jnp.maximum)
    mass = tree([jnp.exp2(t - peak) for t in terms], jnp.add)
    return peak + jnp.log2(mass)


def total(terms):
    return tree(terms, jnp.add)


def kernel(*refs):
    (e_hbm, p_hbm, out, peak_ref, mass_ref, e_ref, p_ref, p3_ref), refs = refs[:8], refs[8:]
    mats, refs = refs[:NCH], refs[NCH:]
    b1s, refs = refs[: len(PARTS)], refs[len(PARTS) :]
    mids, refs = refs[: len(PARTS)], refs[len(PARTS) :]
    b2s, refs = refs[: len(PARTS)], refs[len(PARTS) :]
    (hi_ref, lo_ref, part, wide, peaks, eh2, el2, rb_ref, z_buf, xy_buf, c3x, c3y, sums,
     load_sem, zs, zr, cs, cr, fs, fr, gr) = refs
    dp, bk = lax.axis_index("dp"), lax.axis_index("bucket")
    x, y = lax.div(dp, NY), lax.rem(dp, NY)

    loads_e, loads_p = [], []
    for j in range(NCH):
        rows = pl.ds(CH * j, CH)
        loads_e.append(pltpu.make_async_copy(e_hbm.at[rows], e_ref.at[rows], load_sem.at[j]))
    for q in range(PROT // CH):
        rows = pl.ds(CH * q, CH)
        loads_p.append(pltpu.make_async_copy(p_hbm.at[rows], p_ref.at[rows], load_sem.at[NCH + q]))
    for copy in loads_e[:1] + loads_p + loads_e[1:]:
        copy.start()

    def bk_dev(d):
        return (dp, lax.rem(bk + d, NB))

    def xy_dev(dx, dy):
        return (lax.rem(x + dx, NX) * NY + lax.rem(y + dy, NY), bk)

    xy_peers = sorted(
        [(dx, dy) for dx in range(NX) for dy in range(NY) if dx or dy],
        key=lambda p: -(min(p[0], NX - p[0]) + min(p[1], NY - p[1])),
    )
    bk_peers = sorted(range(1, NB), key=lambda d: -min(d, NB - d))
    x_peers, y_peers = [2, 1, 3], [4, 3, 5, 2, 6, 1, 7]

    barrier = pltpu.get_barrier_semaphore()
    everyone = [bk_dev(d) for d in bk_peers] + [xy_dev(*p) for p in xy_peers]
    for d in everyone:
        pl.semaphore_signal(barrier, 1, device_id=d, device_id_type=MESH)

    def await_bytes(ref, sem):
        pltpu.make_async_copy(ref, ref, sem).wait()

    def send(src, dst, ssem, rsem, device):
        pltpu.make_async_remote_copy(src, dst, ssem, rsem, device_id=device, device_id_type=MESH).start()

    def row_send(n, h, vec):
        z_buf[n, h, bk] = vec
        for d in bk_peers:
            send(z_buf.at[n, h, bk], z_buf.at[n, h, bk], zs.at[2 * n + h], zr.at[2 * n + h], bk_dev(d))

    def row_wait(n, h, combine):
        rest = z_buf.at[n, h, pl.ds(0, NB - 1)]
        await_bytes(rest, zr.at[2 * n + h])
        return combine([z_buf[n, h, d] for d in range(NB)])

    def deep(v, op):
        v = op(op(v.reshape(PROT // 32, 4, 8, CH), axis=0), axis=0)
        return op(v, axis=0, keepdims=True)

    lams = []
    for j in range(NCH + 1):
        if j < NCH:
            loads_e[j].wait()
            eh, el = split(e_ref[CH * j : CH * (j + 1), :])
            e3 = jnp.concatenate([eh, el, eh], axis=1)
            for q in range(PROT // CH):
                r = slice(CH * q, CH * (q + 1))
                if j == 0:
                    loads_p[q].wait()
                    ph, plo = split(p_ref[r, :] * F32(2.0 / math.sqrt(DW) / LN2))
                    p3_ref[r, 0:DW] = ph
                    p3_ref[r, DW : 2 * DW] = ph
                    p3_ref[r, 2 * DW :] = plo
                mats[j][r, :] = nt(p3_ref[r, :], e3)
        if j >= 1:
            v = mats[j - 1][...]
            m = deep(v, jnp.max)
            lam = m + jnp.log2(deep(jnp.exp2(v - m), jnp.sum))
            lams += [lam[:, :128], lam[:, 128:]]
        if j == NCH // 2:
            pl.semaphore_wait(barrier, len(everyone))
            row_send(0, 0, jnp.concatenate(lams, axis=0))
            lams = []
    row_send(0, 1, jnp.concatenate(lams, axis=0))

    def col_send(n, h, rows):
        xy_buf[n, h, dp] = jnp.concatenate(rows, axis=0)
        for p in xy_peers:
            send(xy_buf.at[n, h, dp], xy_buf.at[n, h, dp], cs.at[2 * n + h], cr.at[2 * n + h], xy_dev(*p))

    def col_wait(n, h, combine):
        await_bytes(xy_buf.at[n, h, pl.ds(0, NDP - 1)], cr.at[2 * n + h])
        return combine([xy_buf[n, h, d] for d in range(NDP)])

    def to_row(v, reduce):
        return reduce(v.T, axis=0, keepdims=True)

    def to_tile(row):
        return jnp.broadcast_to(row, (128, 128)).T

    def cut(j):
        return slice(CH * j, CH * (j + 1))

    blocks = [slice(128 * a, 128 * (a + 1)) for a in range(PROT // 128)]
    groups = (range(NCH // 2), range(NCH // 2, NCH))

    def half(h):
        return slice(HALF * h, HALF * (h + 1))

    def spread(h, vec):
        for t in range(8):
            rb_ref[:, HALF * h + 128 * t : HALF * h + 128 * (t + 1)] = vec[t : t + 1, :]

    def row_sums(acc, js, h):
        for r in blocks[4 * h : 4 * h + 4]:
            v = twice(wide[r, :])
            for j in js:
                acc[j] = acc[j] + jnp.sum((mats[j][r, :] * v).reshape(16, 8, CH), axis=0)

    def row_step(n, column):
        acc = [jnp.zeros((8, CH), F32) for _ in mats]
        for h in (0, 1):
            v = column(h)
            for a in range(4):
                wide[blocks[4 * h + a], :] = to_tile(v[a : a + 1, :])
            if h == 0:
                row_sums(acc, range(NCH), 0)
        for h in (0, 1):
            row_sums(acc, groups[h], 1)
            row_send(n, h, jnp.concatenate(
                [jnp.sum(acc[j][:, k : k + 128], axis=0, keepdims=True) for j in groups[h] for k in (0, 128)], axis=0))

    def col_terms(r, js):
        return tree([fold(mats[j][r, :] * rb_ref[:, cut(j)], jnp.add) for j in js], jnp.add)

    def peak_terms(r, js):
        return tree([fold(mats[j][r, :] - rb_ref[:, cut(j)], jnp.maximum) for j in js], jnp.maximum)

    spread(0, row_wait(0, 0, log_sum))
    for r in blocks:
        part[r, :] = peak_terms(r, groups[0])
    spread(1, row_wait(0, 1, log_sum))
    rows_of_peaks = []
    for r in blocks:
        row = to_row(jnp.maximum(part[r, :], peak_terms(r, groups[1])), jnp.max)
        rows_of_peaks.append(row)
        peaks[r, :] = to_tile(row)
    peak = [jnp.concatenate(rows_of_peaks[4 * h : 4 * h + 4], axis=0) for h in (0, 1)]

    masses = []
    for n, r in enumerate(blocks):
        pk = twice(peaks[r, :])
        terms = []
        for j, m in enumerate(mats):
            b = jnp.exp2(m[r, :] - rb_ref[:, cut(j)] - pk)
            m[r, :] = b
            terms.append(fold(b, jnp.add))
        masses.append(rows_of_peaks[n] + jnp.log2(to_row(tree(terms, jnp.add), jnp.sum)))
        if n % 4 == 3:
            col_send(0, n // 4, masses[-4:])

    def halves(g, carry):
        r = pl.ds(pl.multiple_of(g * 64, 64), 64)
        for j, m in enumerate(mats):
            h, l = split(m[r, :])
            hi_ref[r, cut(j)] = h
            lo_ref[r, cut(j)] = l
        return carry

    lax.fori_loop(0, PROT // 64, halves, 0)

    ratio = TOTAL_ROWS / TOTAL_PROT
    g_log, w = [], []

    def first_column(h):
        g_log.append(col_wait(0, h, log_sum))
        w.append(jnp.exp2(peak[h] - g_log[h]))
        return w[h] * ratio

    row_step(1, first_column)
    for a, r in enumerate(blocks):
        peaks[r, :] = to_tile(w[a // 4][a % 4 : a % 4 + 1, :])
    spread(0, 1.0 / row_wait(1, 0, total))
    for r in blocks:
        part[r, :] = col_terms(r, groups[0])
    spread(1, 1.0 / row_wait(1, 1, total))
    for h in (0, 1):
        rows = [to_row(part[r, :] + col_terms(r, groups[1]), jnp.sum) for r in blocks[4 * h : 4 * h + 4]]
        col_send(1, h, [w[h][a : a + 1, :] * row for a, row in enumerate(rows)])
    row_step(2, lambda h: w[h] * ratio / col_wait(1, h, total))
    w, g_log = jnp.concatenate(w, axis=0), jnp.concatenate(g_log, axis=0)

    def scale_rows(h):
        for a in range(8 * h, 8 * h + 8):
            r = slice(128 * a, 128 * (a + 1))
            t, l = split(e_ref[r, :] * twice(to_tile(rb_ref[:, r])))
            eh2[r, :] = t
            el2[r, :] = l

    def product(r, k):
        h = hi_ref[r, k]
        return nn(h, eh2[k, :]) + nn(h, el2[k, :]) + nn(lo_ref[r, k], eh2[k, :])

    spread(0, 1.0 / row_wait(2, 0, total))
    scale_rows(0)
    first = slice(PARTS[0][0], PARTS[0][0] + PARTS[0][1])
    sums[first, :] = product(first, half(0))
    spread(1, 1.0 / row_wait(2, 1, total))
    scale_rows(1)

    def rows_of(base, unit, index):
        return pl.ds(pl.multiple_of(base + unit * index, 8), unit)

    n_x, n_y = (NX, x, x_peers, lambda d: xy_dev(d, 0)), (NY, y, y_peers, lambda d: xy_dev(0, d))

    def plan(p):
        base, size, first = PARTS[p]
        one, two = (n_x, n_y) if first == "x" else (n_y, n_x)
        return base, size, one, two, size // one[0], size // NDP

    def scatter_one(p):
        base, size, (n, me, peers, dev), _, c1, _ = plan(p)
        for d in peers:
            send(sums.at[rows_of(base, c1, lax.rem(me + d, n))], b1s[p].at[me], fs.at[4 * p], fr.at[4 * p], dev(d))
        b1s[p][me] = sums[rows_of(base, c1, me), :]

    def scatter_two(p):
        _, size, (n1, _, _, _), (n, me, peers, dev), c1, c2 = plan(p)
        await_bytes(b1s[p].at[pl.ds(0, n1 - 1)], fr.at[4 * p])
        mids[p][...] = total([b1s[p][d] for d in range(n1)])
        for d in peers:
            send(mids[p].at[rows_of(0, c2, lax.rem(me + d, n))], b2s[p].at[me], fs.at[4 * p + 1], fr.at[4 * p + 1], dev(d))
        b2s[p][me] = mids[p][rows_of(0, c2, me), :]

    def gather_one(p):
        base, size, (_, me1, _, _), (n, me, peers, dev), c1, c2 = plan(p)
        await_bytes(b2s[p].at[pl.ds(0, n - 1)], fr.at[4 * p + 1])
        own = rows_of(base, c2, me1 * n + me)
        v = total([b2s[p][d] for d in range(n)]) * twice(part[own, :])
        out[own, :] = v * lax.rsqrt(jnp.mean(v * v, axis=1, keepdims=True) + 1e-06)
        for d in peers:
            arrived = fr.at[4 * p + 2] if PARTS[p][2] == "y" else gr.at[NY * p + d]
            send(out.at[own], out.at[own], fs.at[4 * p + 2], arrived, dev(d))
        if PARTS[p][2] == "x":
            for d in x_peers:
                send(out.at[own], out.at[own], fs.at[4 * p + 3], fr.at[4 * p + 3], xy_dev(d, 0))

    def gather_two(p):
        base, size, (_, me, peers, dev), _, c1, c2 = plan(p)
        if PARTS[p][2] == "y":
            await_bytes(out.at[pl.ds(0, c1 - c2)], fr.at[4 * p + 2])
            mid = rows_of(base, c1, me)
            for d in peers:
                send(out.at[mid], out.at[mid], fs.at[4 * p + 3], fr.at[4 * p + 3], dev(d))
            return
        for e in (1, 7, 2, 6, 3, 5, 4):
            got = rows_of(base + c1 * x, c2, lax.rem(y + NY - e, NY))
            await_bytes(out.at[got], gr.at[NY * p + e])
            for d in x_peers:
                send(out.at[got], out.at[got], fs.at[4 * p + 3], fr.at[4 * p + 3], xy_dev(d, 0))

    for p, (base, size, _) in enumerate(PARTS):
        rows = slice(base, base + size)
        acc = sums[rows, :] + product(rows, half(1)) if p == 0 else product(rows, slice(0, ROWS))
        sums[rows, :] = acc * twice(peaks[rows, :])
        scatter_one(p)
        if p == 2:
            c3x[x] = w * jnp.concatenate([to_row(col_terms(r, range(NCH)), jnp.sum) for r in blocks], axis=0)
            for d in x_peers:
                send(c3x.at[x], c3x.at[x], cs.at[4], cr.at[4], xy_dev(d, 0))

    scatter_two(1)
    await_bytes(c3x.at[pl.ds(0, NX - 1)], cr.at[4])
    c3y[y] = total([c3x[d] for d in range(NX)])
    for d in y_peers:
        send(c3y.at[y], c3y.at[y], cs.at[5], cr.at[5], xy_dev(0, d))
    scatter_two(2)
    scatter_two(0)
    scatter_two(3)
    await_bytes(c3y.at[pl.ds(0, NY - 1)], cr.at[5])
    mass = total([c3y[d] for d in range(NY)])
    peak_ref[...] = (LN2 * g_log).reshape(peak_ref.shape)
    mass_ref[...] = jnp.log(mass).reshape(mass_ref.shape)
    for a, r in enumerate(blocks):
        part[r, :] = to_tile(1.0 / mass[a : a + 1, :])
    for p in (1, 0, 2, 3):
        gather_one(p)
    for p in (0, 1, 2, 3):
        gather_two(p)
    for p in (0, 1, 2, 3):
        _, size, _, _, c1, c2 = plan(p)
        await_bytes(out.at[pl.ds(0, size - c1)], fr.at[4 * p + 3])
        for n, sent in enumerate((size - c1, c1 - c2, c1 - c2, size - c1)):
            await_bytes(sums.at[pl.ds(0, sent)], fs.at[4 * p + n])

    for n in range(4):
        await_bytes(xy_buf.at[n // 2, n % 2, pl.ds(0, NDP - 1)], cs.at[n])
    for n in range(6):
        await_bytes(z_buf.at[n // 2, n % 2, pl.ds(0, NB - 1)], zs.at[n])
    await_bytes(c3x.at[pl.ds(0, NX - 1)], cs.at[4])
    await_bytes(c3y.at[pl.ds(0, NY - 1)], cs.at[5])


def body(embeddings, prototypes):
    vm = pltpu.VMEM
    dma = pltpu.SemaphoreType.DMA
    counts = [(NX, NY) if first == "x" else (NY, NX) for _, _, first in PARTS]
    sizes = [size for _, size, _ in PARTS]
    new_protos, peak, mass = pl.pallas_call(
        kernel,
        out_shape=(pltpu.VMEM((PROT, DW), F32), pltpu.VMEM((PROT,), F32), pltpu.VMEM((PROT,), F32)),
        in_specs=[pl.BlockSpec(memory_space=pl.ANY)] * 2,
        out_specs=(pl.BlockSpec(memory_space=vm),) * 3,
        scratch_shapes=[
            vm((ROWS, DW), F32),
            vm((PROT, DW), F32),
            vm((PROT, 3 * DW), BF16),
            *[vm((PROT, CH), F32) for _ in range(NCH)],
            *[vm((a, s // a, DW), F32) for (a, _), s in zip(counts, sizes)],
            *[vm((s // a, DW), F32) for (a, _), s in zip(counts, sizes)],
            *[vm((b, s // NDP, DW), F32) for (_, b), s in zip(counts, sizes)],
            vm((PROT, ROWS), BF16),
            vm((PROT, ROWS), BF16),
            vm((PROT, 128), F32),
            vm((PROT, 128), F32),
            vm((PROT, 128), F32),
            vm((ROWS, DW), BF16),
            vm((ROWS, DW), BF16),
            vm((1, ROWS), F32),
            vm((3, 2, NB, 8, 128), F32),
            vm((2, 2, NDP, 4, 128), F32),
            vm((NX, 8, 128), F32),
            vm((NY, 8, 128), F32),
            vm((PROT, DW), F32),
            dma((NCH + PROT // CH,)),
            dma((6,)), dma((6,)),
            dma((6,)), dma((6,)),
            dma((4 * len(PARTS),)), dma((4 * len(PARTS),)), dma((NY * len(PARTS),)),
        ],
        compiler_params=pltpu.CompilerParams(
            collective_id=0, has_side_effects=True, vmem_limit_bytes=56 * 1024 * 1024),
        name="sinkhorn",
    )(embeddings, prototypes)
    return new_protos, (math.log(TOTAL_ROWS / TOTAL_PROT) - peak) - mass


def solution(mesh):
    in_specs = (P("dp", None), P("bucket", None))
    out_specs = (P("bucket", None), P("bucket"))
    return jax.shard_map(body, mesh=mesh, in_specs=in_specs, out_specs=out_specs, check_vma=False)
```

```python
import math

import jax
import jax.numpy as jnp
from jax import lax
from jax.experimental import pallas as pl
from jax.experimental.pallas import tpu as pltpu
from jax.sharding import PartitionSpec as P

NX, NY, NZ, NC = 4, 8, 8, 2
NDP = NX * NY
MESH = pl.DeviceIdType.MESH
F32 = jnp.float32
BF16 = jnp.bfloat16
LN2 = math.log(2.0)

ROWS = 2048
PROT = 1024
DW = 256
TOTAL_ROWS = ROWS * NDP
TOTAL_PROT = PROT * NZ * NC

CH = 256
NCH = ROWS // CH
HALF = ROWS // 2
NB = NZ * NC
PARTS = ((0, 256, "y"), (256, 256, "x"), (512, 256, "x"), (768, 256, "x"))


def split(x):
    hi = x.astype(BF16)
    return hi, (x - hi.astype(F32)).astype(BF16)


def nt(a, b):
    return lax.dot_general(a, b, (((1,), (1,)), ((), ())), preferred_element_type=F32)


def nn(a, b):
    return lax.dot_general(a, b, (((1,), (0,)), ((), ())), preferred_element_type=F32)


def tree(parts, op):
    while len(parts) > 1:
        parts = [op(a, b) for a, b in zip(parts[::2], parts[1::2])]
    return parts[0]


def twice(v):
    return jnp.concatenate([v, v], axis=1)


def fold(v, op):
    return op(v[:, :128], v[:, 128:])


def log_sum(terms):
    peak = tree(terms, jnp.maximum)
    mass = tree([jnp.exp2(t - peak) for t in terms], jnp.add)
    return peak + jnp.log2(mass)


def total(terms):
    return tree(terms, jnp.add)


def kernel(*refs):
    (e_hbm, p_hbm, out, pot_ref, e_ref, p_ref, p3_ref), refs = refs[:7], refs[7:]
    mats, refs = refs[:NCH], refs[NCH:]
    b1s, refs = refs[: len(PARTS)], refs[len(PARTS) :]
    mids, refs = refs[: len(PARTS)], refs[len(PARTS) :]
    b2s, refs = refs[: len(PARTS)], refs[len(PARTS) :]
    (hi_ref, lo_ref, part, wide, peaks, eh2, el2, rb_ref, z_buf, xy_buf, c3x, c3y, sums,
     load_sem, zs, zr, cs, cr, fs, fr, gr) = refs
    dp, bk = lax.axis_index("dp"), lax.axis_index("bucket")
    x, y = lax.div(dp, NY), lax.rem(dp, NY)

    loads_e, loads_p = [], []
    for j in range(NCH):
        rows = pl.ds(CH * j, CH)
        loads_e.append(pltpu.make_async_copy(e_hbm.at[rows], e_ref.at[rows], load_sem.at[j]))
    for q in range(PROT // CH):
        rows = pl.ds(CH * q, CH)
        loads_p.append(pltpu.make_async_copy(p_hbm.at[rows], p_ref.at[rows], load_sem.at[NCH + q]))
    for copy in loads_e[:1] + loads_p + loads_e[1:]:
        copy.start()

    def bk_dev(d):
        return (dp, lax.rem(bk + d, NB))

    def xy_dev(dx, dy):
        return (lax.rem(x + dx, NX) * NY + lax.rem(y + dy, NY), bk)

    xy_peers = sorted(
        [(dx, dy) for dx in range(NX) for dy in range(NY) if dx or dy],
        key=lambda p: -(min(p[0], NX - p[0]) + min(p[1], NY - p[1])),
    )
    bk_peers = sorted(range(1, NB), key=lambda d: -min(d, NB - d))
    x_peers, y_peers = [2, 1, 3], [4, 3, 5, 2, 6, 1, 7]

    barrier = pltpu.get_barrier_semaphore()
    everyone = [bk_dev(d) for d in bk_peers] + [xy_dev(*p) for p in xy_peers]
    for d in everyone:
        pl.semaphore_signal(barrier, 1, device_id=d, device_id_type=MESH)

    def await_bytes(ref, sem):
        pltpu.make_async_copy(ref, ref, sem).wait()

    def send(src, dst, ssem, rsem, device):
        pltpu.make_async_remote_copy(src, dst, ssem, rsem, device_id=device, device_id_type=MESH).start()

    def row_send(n, h, vec):
        z_buf[n, h, bk] = vec
        for d in bk_peers:
            send(z_buf.at[n, h, bk], z_buf.at[n, h, bk], zs.at[2 * n + h], zr.at[2 * n + h], bk_dev(d))

    def row_wait(n, h, combine):
        rest = z_buf.at[n, h, pl.ds(0, NB - 1)]
        await_bytes(rest, zr.at[2 * n + h])
        return combine([z_buf[n, h, d] for d in range(NB)])

    def deep(v, op):
        v = op(op(v.reshape(PROT // 32, 4, 8, CH), axis=0), axis=0)
        return op(v, axis=0, keepdims=True)

    lams = []
    for j in range(NCH + 1):
        if j < NCH:
            loads_e[j].wait()
            eh, el = split(e_ref[CH * j : CH * (j + 1), :])
            e3 = jnp.concatenate([eh, el, eh], axis=1)
            for q in range(PROT // CH):
                r = slice(CH * q, CH * (q + 1))
                if j == 0:
                    loads_p[q].wait()
                    ph, plo = split(p_ref[r, :] * F32(2.0 / math.sqrt(DW) / LN2))
                    p3_ref[r, 0:DW] = ph
                    p3_ref[r, DW : 2 * DW] = ph
                    p3_ref[r, 2 * DW :] = plo
                mats[j][r, :] = nt(p3_ref[r, :], e3)
        if j >= 1:
            v = mats[j - 1][...]
            m = deep(v, jnp.max)
            lam = m + jnp.log2(deep(jnp.exp2(v - m), jnp.sum))
            lams += [lam[:, :128], lam[:, 128:]]
        if j == NCH // 2:
            pl.semaphore_wait(barrier, len(everyone))
            row_send(0, 0, jnp.concatenate(lams, axis=0))
            lams = []
    row_send(0, 1, jnp.concatenate(lams, axis=0))

    def col_send(n, h, rows):
        xy_buf[n, h, dp] = jnp.concatenate(rows, axis=0)
        for p in xy_peers:
            send(xy_buf.at[n, h, dp], xy_buf.at[n, h, dp], cs.at[2 * n + h], cr.at[2 * n + h], xy_dev(*p))

    def col_wait(n, h, combine):
        await_bytes(xy_buf.at[n, h, pl.ds(0, NDP - 1)], cr.at[2 * n + h])
        return combine([xy_buf[n, h, d] for d in range(NDP)])

    def to_row(v, reduce):
        return reduce(v.T, axis=0, keepdims=True)

    def to_tile(row):
        return jnp.broadcast_to(row, (128, 128)).T

    def cut(j):
        return slice(CH * j, CH * (j + 1))

    blocks = [slice(128 * a, 128 * (a + 1)) for a in range(PROT // 128)]
    groups = (range(NCH // 2), range(NCH // 2, NCH))

    def half(h):
        return slice(HALF * h, HALF * (h + 1))

    def spread(h, vec):
        for t in range(8):
            rb_ref[:, HALF * h + 128 * t : HALF * h + 128 * (t + 1)] = vec[t : t + 1, :]

    def row_sums(acc, js, h):
        for r in blocks[4 * h : 4 * h + 4]:
            v = twice(wide[r, :])
            for j in js:
                acc[j] = acc[j] + jnp.sum((mats[j][r, :] * v).reshape(16, 8, CH), axis=0)

    def row_step(n, column):
        acc = [jnp.zeros((8, CH), F32) for _ in mats]
        for h in (0, 1):
            v = column(h)
            for a in range(4):
                wide[blocks[4 * h + a], :] = to_tile(v[a : a + 1, :])
            if h == 0:
                row_sums(acc, range(NCH), 0)
        for h in (0, 1):
            row_sums(acc, groups[h], 1)
            row_send(n, h, jnp.concatenate(
                [jnp.sum(acc[j][:, k : k + 128], axis=0, keepdims=True) for j in groups[h] for k in (0, 128)], axis=0))

    def col_terms(r, js):
        return tree([fold(mats[j][r, :] * rb_ref[:, cut(j)], jnp.add) for j in js], jnp.add)

    def peak_terms(r, js):
        return tree([fold(mats[j][r, :] - rb_ref[:, cut(j)], jnp.maximum) for j in js], jnp.maximum)

    spread(0, row_wait(0, 0, log_sum))
    for r in blocks:
        part[r, :] = peak_terms(r, groups[0])
    spread(1, row_wait(0, 1, log_sum))
    rows_of_peaks = []
    for r in blocks:
        row = to_row(jnp.maximum(part[r, :], peak_terms(r, groups[1])), jnp.max)
        rows_of_peaks.append(row)
        peaks[r, :] = to_tile(row)
    peak = [jnp.concatenate(rows_of_peaks[4 * h : 4 * h + 4], axis=0) for h in (0, 1)]

    masses = []
    for n, r in enumerate(blocks):
        pk = twice(peaks[r, :])
        terms = []
        for j, m in enumerate(mats):
            b = jnp.exp2(m[r, :] - rb_ref[:, cut(j)] - pk)
            m[r, :] = b
            terms.append(fold(b, jnp.add))
        masses.append(rows_of_peaks[n] + jnp.log2(to_row(tree(terms, jnp.add), jnp.sum)))
        if n % 4 == 3:
            col_send(0, n // 4, masses[-4:])

    def halves(g, carry):
        r = pl.ds(pl.multiple_of(g * 64, 64), 64)
        for j, m in enumerate(mats):
            h, l = split(m[r, :])
            hi_ref[r, cut(j)] = h
            lo_ref[r, cut(j)] = l
        return carry

    lax.fori_loop(0, PROT // 64, halves, 0)

    ratio = TOTAL_ROWS / TOTAL_PROT
    g_log, w = [], []

    def first_column(h):
        g_log.append(col_wait(0, h, log_sum))
        w.append(jnp.exp2(peak[h] - g_log[h]))
        return w[h] * ratio

    row_step(1, first_column)
    for a, r in enumerate(blocks):
        peaks[r, :] = to_tile(w[a // 4][a % 4 : a % 4 + 1, :])
    spread(0, 1.0 / row_wait(1, 0, total))
    for r in blocks:
        part[r, :] = col_terms(r, groups[0])
    spread(1, 1.0 / row_wait(1, 1, total))
    for h in (0, 1):
        rows = [to_row(part[r, :] + col_terms(r, groups[1]), jnp.sum) for r in blocks[4 * h : 4 * h + 4]]
        col_send(1, h, [w[h][a : a + 1, :] * row for a, row in enumerate(rows)])
    row_step(2, lambda h: w[h] * ratio / col_wait(1, h, total))
    w, g_log = jnp.concatenate(w, axis=0), jnp.concatenate(g_log, axis=0)

    def scale_rows(h):
        for a in range(8 * h, 8 * h + 8):
            r = slice(128 * a, 128 * (a + 1))
            t, l = split(e_ref[r, :] * twice(to_tile(rb_ref[:, r])))
            eh2[r, :] = t
            el2[r, :] = l

    def product(r, k):
        h = hi_ref[r, k]
        return nn(h, eh2[k, :]) + nn(h, el2[k, :]) + nn(lo_ref[r, k], eh2[k, :])

    spread(0, 1.0 / row_wait(2, 0, total))
    scale_rows(0)
    first = slice(PARTS[0][0], PARTS[0][0] + PARTS[0][1])
    sums[first, :] = product(first, half(0))
    spread(1, 1.0 / row_wait(2, 1, total))
    scale_rows(1)

    def rows_of(base, unit, index):
        return pl.ds(pl.multiple_of(base + unit * index, 8), unit)

    n_x, n_y = (NX, x, x_peers, lambda d: xy_dev(d, 0)), (NY, y, y_peers, lambda d: xy_dev(0, d))

    def plan(p):
        base, size, first = PARTS[p]
        one, two = (n_x, n_y) if first == "x" else (n_y, n_x)
        return base, size, one, two, size // one[0], size // NDP

    def scatter_one(p):
        base, size, (n, me, peers, dev), _, c1, _ = plan(p)
        for d in peers:
            send(sums.at[rows_of(base, c1, lax.rem(me + d, n))], b1s[p].at[me], fs.at[4 * p], fr.at[4 * p], dev(d))
        b1s[p][me] = sums[rows_of(base, c1, me), :]

    def scatter_two(p):
        _, size, (n1, _, _, _), (n, me, peers, dev), c1, c2 = plan(p)
        await_bytes(b1s[p].at[pl.ds(0, n1 - 1)], fr.at[4 * p])
        mids[p][...] = total([b1s[p][d] for d in range(n1)])
        for d in peers:
            send(mids[p].at[rows_of(0, c2, lax.rem(me + d, n))], b2s[p].at[me], fs.at[4 * p + 1], fr.at[4 * p + 1], dev(d))
        b2s[p][me] = mids[p][rows_of(0, c2, me), :]

    def gather_one(p):
        base, size, (_, me1, _, _), (n, me, peers, dev), c1, c2 = plan(p)
        await_bytes(b2s[p].at[pl.ds(0, n - 1)], fr.at[4 * p + 1])
        own = rows_of(base, c2, me1 * n + me)
        v = total([b2s[p][d] for d in range(n)]) * twice(part[own, :])
        out[own, :] = v * lax.rsqrt(jnp.mean(v * v, axis=1, keepdims=True) + 1e-06)
        for d in peers:
            arrived = fr.at[4 * p + 2] if PARTS[p][2] == "y" else gr.at[NY * p + d]
            send(out.at[own], out.at[own], fs.at[4 * p + 2], arrived, dev(d))
        if PARTS[p][2] == "x":
            for d in x_peers:
                send(out.at[own], out.at[own], fs.at[4 * p + 3], fr.at[4 * p + 3], xy_dev(d, 0))

    def gather_two(p):
        base, size, (_, me, peers, dev), _, c1, c2 = plan(p)
        if PARTS[p][2] == "y":
            await_bytes(out.at[pl.ds(0, c1 - c2)], fr.at[4 * p + 2])
            mid = rows_of(base, c1, me)
            for d in peers:
                send(out.at[mid], out.at[mid], fs.at[4 * p + 3], fr.at[4 * p + 3], dev(d))
            return
        for e in (1, 7, 2, 6, 3, 5, 4):
            got = rows_of(base + c1 * x, c2, lax.rem(y + NY - e, NY))
            await_bytes(out.at[got], gr.at[NY * p + e])
            for d in x_peers:
                send(out.at[got], out.at[got], fs.at[4 * p + 3], fr.at[4 * p + 3], xy_dev(d, 0))

    for p, (base, size, _) in enumerate(PARTS):
        rows = slice(base, base + size)
        acc = sums[rows, :] + product(rows, half(1)) if p == 0 else product(rows, slice(0, ROWS))
        sums[rows, :] = acc * twice(peaks[rows, :])
        scatter_one(p)
        if p == 2:
            c3x[x] = w * jnp.concatenate([to_row(col_terms(r, range(NCH)), jnp.sum) for r in blocks], axis=0)
            for d in x_peers:
                send(c3x.at[x], c3x.at[x], cs.at[4], cr.at[4], xy_dev(d, 0))

    scatter_two(1)
    await_bytes(c3x.at[pl.ds(0, NX - 1)], cr.at[4])
    c3y[y] = total([c3x[d] for d in range(NX)])
    for d in y_peers:
        send(c3y.at[y], c3y.at[y], cs.at[5], cr.at[5], xy_dev(0, d))
    scatter_two(0)
    scatter_two(2)
    scatter_two(3)
    await_bytes(c3y.at[pl.ds(0, NY - 1)], cr.at[5])
    mass = total([c3y[d] for d in range(NY)])
    pot_ref[...] = ((math.log(TOTAL_ROWS / TOTAL_PROT) - LN2 * g_log) - jnp.log(mass)).reshape(pot_ref.shape)
    for a, r in enumerate(blocks):
        part[r, :] = to_tile(1.0 / mass[a : a + 1, :])
    for p in (1, 0, 2, 3):
        gather_one(p)
    for p in (1, 2, 3, 0):
        gather_two(p)
    for p in (0, 1, 2, 3):
        _, size, _, _, c1, c2 = plan(p)
        await_bytes(out.at[pl.ds(0, size - c1)], fr.at[4 * p + 3])
        for n, sent in enumerate((size - c1, c1 - c2, c1 - c2, size - c1)):
            await_bytes(sums.at[pl.ds(0, sent)], fs.at[4 * p + n])

    for n in range(4):
        await_bytes(xy_buf.at[n // 2, n % 2, pl.ds(0, NDP - 1)], cs.at[n])
    for n in range(6):
        await_bytes(z_buf.at[n // 2, n % 2, pl.ds(0, NB - 1)], zs.at[n])
    await_bytes(c3x.at[pl.ds(0, NX - 1)], cs.at[4])
    await_bytes(c3y.at[pl.ds(0, NY - 1)], cs.at[5])


def body(embeddings, prototypes):
    vm = pltpu.VMEM
    dma = pltpu.SemaphoreType.DMA
    counts = [(NX, NY) if first == "x" else (NY, NX) for _, _, first in PARTS]
    sizes = [size for _, size, _ in PARTS]
    new_protos, pot = pl.pallas_call(
        kernel,
        out_shape=(pltpu.VMEM((PROT, DW), F32), pltpu.VMEM((PROT,), F32)),
        in_specs=[pl.BlockSpec(memory_space=pl.ANY)] * 2,
        out_specs=(pl.BlockSpec(memory_space=vm), pl.BlockSpec(memory_space=vm)),
        scratch_shapes=[
            vm((ROWS, DW), F32),
            vm((PROT, DW), F32),
            vm((PROT, 3 * DW), BF16),
            *[vm((PROT, CH), F32) for _ in range(NCH)],
            *[vm((a, s // a, DW), F32) for (a, _), s in zip(counts, sizes)],
            *[vm((s // a, DW), F32) for (a, _), s in zip(counts, sizes)],
            *[vm((b, s // NDP, DW), F32) for (_, b), s in zip(counts, sizes)],
            vm((PROT, ROWS), BF16),
            vm((PROT, ROWS), BF16),
            vm((PROT, 128), F32),
            vm((PROT, 128), F32),
            vm((PROT, 128), F32),
            vm((ROWS, DW), BF16),
            vm((ROWS, DW), BF16),
            vm((1, ROWS), F32),
            vm((3, 2, NB, 8, 128), F32),
            vm((2, 2, NDP, 4, 128), F32),
            vm((NX, 8, 128), F32),
            vm((NY, 8, 128), F32),
            vm((PROT, DW), F32),
            dma((NCH + PROT // CH,)),
            dma((6,)), dma((6,)),
            dma((6,)), dma((6,)),
            dma((4 * len(PARTS),)), dma((4 * len(PARTS),)), dma((NY * len(PARTS),)),
        ],
        compiler_params=pltpu.CompilerParams(
            collective_id=0, has_side_effects=True, vmem_limit_bytes=56 * 1024 * 1024),
        name="sinkhorn",
    )(embeddings, prototypes)
    return new_protos, pot


def solution(mesh):
    in_specs = (P("dp", None), P("bucket", None))
    out_specs = (P("bucket", None), P("bucket"))
    return jax.shard_map(body, mesh=mesh, in_specs=in_specs, out_specs=out_specs, check_vma=False)
```

```python
import math

import jax
import jax.numpy as jnp
from jax import lax
from jax.experimental import pallas as pl
from jax.experimental.pallas import tpu as pltpu
from jax.sharding import PartitionSpec as P

NX, NY, NZ, NC = 4, 8, 8, 2
NDP = NX * NY
MESH = pl.DeviceIdType.MESH
F32 = jnp.float32
BF16 = jnp.bfloat16
LN2 = math.log(2.0)

ROWS = 2048
PROT = 1024
DW = 256
TOTAL_ROWS = ROWS * NDP
TOTAL_PROT = PROT * NZ * NC

CH = 256
NCH = ROWS // CH
HALF = ROWS // 2
NB = NZ * NC
PARTS = ((0, 256, "y"), (256, 256, "x"), (512, 256, "x"), (768, 256, "x"))


def split(x):
    hi = x.astype(BF16)
    return hi, (x - hi.astype(F32)).astype(BF16)


def nt(a, b):
    return lax.dot_general(a, b, (((1,), (1,)), ((), ())), preferred_element_type=F32)


def nn(a, b):
    return lax.dot_general(a, b, (((1,), (0,)), ((), ())), preferred_element_type=F32)


def tree(parts, op):
    while len(parts) > 1:
        parts = [op(a, b) for a, b in zip(parts[::2], parts[1::2])]
    return parts[0]


def twice(v):
    return jnp.concatenate([v, v], axis=1)


def fold(v, op):
    return op(v[:, :128], v[:, 128:])


def log_sum(terms):
    peak = tree(terms, jnp.maximum)
    mass = tree([jnp.exp2(t - peak) for t in terms], jnp.add)
    return peak + jnp.log2(mass)


def total(terms):
    return tree(terms, jnp.add)


def kernel(*refs):
    (e_hbm, p_hbm, out, pot_ref, e_ref, p_ref, p3_ref), refs = refs[:7], refs[7:]
    mats, refs = refs[:NCH], refs[NCH:]
    b1s, refs = refs[: len(PARTS)], refs[len(PARTS) :]
    mids, refs = refs[: len(PARTS)], refs[len(PARTS) :]
    b2s, refs = refs[: len(PARTS)], refs[len(PARTS) :]
    (hi_ref, lo_ref, part, wide, peaks, eh2, el2, rb_ref, z_buf, xy_buf, c3x, c3y, sums,
     load_sem, zs, zr, cs, cr, fs, fr, gr) = refs
    dp, bk = lax.axis_index("dp"), lax.axis_index("bucket")
    x, y = lax.div(dp, NY), lax.rem(dp, NY)

    loads_e, loads_p = [], []
    for j in range(NCH):
        rows = pl.ds(CH * j, CH)
        loads_e.append(pltpu.make_async_copy(e_hbm.at[rows], e_ref.at[rows], load_sem.at[j]))
    for q in range(PROT // CH):
        rows = pl.ds(CH * q, CH)
        loads_p.append(pltpu.make_async_copy(p_hbm.at[rows], p_ref.at[rows], load_sem.at[NCH + q]))
    for copy in loads_e[:1] + loads_p + loads_e[1:]:
        copy.start()

    def bk_dev(d):
        return (dp, lax.rem(bk + d, NB))

    def xy_dev(dx, dy):
        return (lax.rem(x + dx, NX) * NY + lax.rem(y + dy, NY), bk)

    xy_peers = sorted(
        [(dx, dy) for dx in range(NX) for dy in range(NY) if dx or dy],
        key=lambda p: -(min(p[0], NX - p[0]) + min(p[1], NY - p[1])),
    )
    bk_peers = sorted(range(1, NB), key=lambda d: -min(d, NB - d))
    x_peers, y_peers = [2, 1, 3], [4, 3, 5, 2, 6, 1, 7]

    barrier = pltpu.get_barrier_semaphore()
    everyone = [bk_dev(d) for d in bk_peers] + [xy_dev(*p) for p in xy_peers]
    for d in everyone:
        pl.semaphore_signal(barrier, 1, device_id=d, device_id_type=MESH)

    def await_bytes(ref, sem):
        pltpu.make_async_copy(ref, ref, sem).wait()

    def send(src, dst, ssem, rsem, device):
        pltpu.make_async_remote_copy(src, dst, ssem, rsem, device_id=device, device_id_type=MESH).start()

    def row_send(n, h, vec):
        z_buf[n, h, bk] = vec
        for d in bk_peers:
            send(z_buf.at[n, h, bk], z_buf.at[n, h, bk], zs.at[2 * n + h], zr.at[2 * n + h], bk_dev(d))

    def row_wait(n, h, combine):
        rest = z_buf.at[n, h, pl.ds(0, NB - 1)]
        await_bytes(rest, zr.at[2 * n + h])
        return combine([z_buf[n, h, d] for d in range(NB)])

    def deep(v, op):
        v = op(op(v.reshape(PROT // 32, 4, 8, CH), axis=0), axis=0)
        return op(v, axis=0, keepdims=True)

    lams = []
    for j in range(NCH + 1):
        if j < NCH:
            loads_e[j].wait()
            eh, el = split(e_ref[CH * j : CH * (j + 1), :])
            e3 = jnp.concatenate([eh, el, eh], axis=1)
            for q in range(PROT // CH):
                r = slice(CH * q, CH * (q + 1))
                if j == 0:
                    loads_p[q].wait()
                    ph, plo = split(p_ref[r, :] * F32(2.0 / math.sqrt(DW) / LN2))
                    p3_ref[r, 0:DW] = ph
                    p3_ref[r, DW : 2 * DW] = ph
                    p3_ref[r, 2 * DW :] = plo
                mats[j][r, :] = nt(p3_ref[r, :], e3)
        if j >= 1:
            v = mats[j - 1][...]
            m = deep(v, jnp.max)
            lam = m + jnp.log2(deep(jnp.exp2(v - m), jnp.sum))
            lams += [lam[:, :128], lam[:, 128:]]
        if j == NCH // 2:
            pl.semaphore_wait(barrier, len(everyone))
            row_send(0, 0, jnp.concatenate(lams, axis=0))
            lams = []
    row_send(0, 1, jnp.concatenate(lams, axis=0))

    def col_send(n, h, rows):
        xy_buf[n, h, dp] = jnp.concatenate(rows, axis=0)
        for p in xy_peers:
            send(xy_buf.at[n, h, dp], xy_buf.at[n, h, dp], cs.at[2 * n + h], cr.at[2 * n + h], xy_dev(*p))

    def col_wait(n, h, combine):
        await_bytes(xy_buf.at[n, h, pl.ds(0, NDP - 1)], cr.at[2 * n + h])
        return combine([xy_buf[n, h, d] for d in range(NDP)])

    def to_row(v, reduce):
        return reduce(v.T, axis=0, keepdims=True)

    def to_tile(row):
        return jnp.broadcast_to(row, (128, 128)).T

    def cut(j):
        return slice(CH * j, CH * (j + 1))

    blocks = [slice(128 * a, 128 * (a + 1)) for a in range(PROT // 128)]
    groups = (range(NCH // 2), range(NCH // 2, NCH))

    def half(h):
        return slice(HALF * h, HALF * (h + 1))

    def spread(h, vec):
        for t in range(8):
            rb_ref[:, HALF * h + 128 * t : HALF * h + 128 * (t + 1)] = vec[t : t + 1, :]

    def row_sums(acc, js, h):
        for r in blocks[4 * h : 4 * h + 4]:
            v = twice(wide[r, :])
            for j in js:
                acc[j] = acc[j] + jnp.sum((mats[j][r, :] * v).reshape(16, 8, CH), axis=0)

    def row_step(n, column):
        acc = [jnp.zeros((8, CH), F32) for _ in mats]
        for h in (0, 1):
            v = column(h)
            for a in range(4):
                wide[blocks[4 * h + a], :] = to_tile(v[a : a + 1, :])
            if h == 0:
                row_sums(acc, range(NCH), 0)
        for h in (0, 1):
            row_sums(acc, groups[h], 1)
            row_send(n, h, jnp.concatenate(
                [jnp.sum(acc[j][:, k : k + 128], axis=0, keepdims=True) for j in groups[h] for k in (0, 128)], axis=0))

    def col_terms(r, js):
        return tree([fold(mats[j][r, :] * rb_ref[:, cut(j)], jnp.add) for j in js], jnp.add)

    def peak_terms(r, js):
        return tree([fold(mats[j][r, :] - rb_ref[:, cut(j)], jnp.maximum) for j in js], jnp.maximum)

    spread(0, row_wait(0, 0, log_sum))
    for r in blocks:
        part[r, :] = peak_terms(r, groups[0])
    spread(1, row_wait(0, 1, log_sum))
    rows_of_peaks = []
    for r in blocks:
        row = to_row(jnp.maximum(part[r, :], peak_terms(r, groups[1])), jnp.max)
        rows_of_peaks.append(row)
        peaks[r, :] = to_tile(row)
    peak = [jnp.concatenate(rows_of_peaks[4 * h : 4 * h + 4], axis=0) for h in (0, 1)]

    masses = []
    for n, r in enumerate(blocks):
        pk = twice(peaks[r, :])
        terms = []
        for j, m in enumerate(mats):
            b = jnp.exp2(m[r, :] - rb_ref[:, cut(j)] - pk)
            m[r, :] = b
            terms.append(fold(b, jnp.add))
        masses.append(rows_of_peaks[n] + jnp.log2(to_row(tree(terms, jnp.add), jnp.sum)))
        if n % 4 == 3:
            col_send(0, n // 4, masses[-4:])

    def halves(g, carry):
        r = pl.ds(pl.multiple_of(g * 64, 64), 64)
        for j, m in enumerate(mats):
            h, l = split(m[r, :])
            hi_ref[r, cut(j)] = h
            lo_ref[r, cut(j)] = l
        return carry

    lax.fori_loop(0, PROT // 64, halves, 0)

    ratio = TOTAL_ROWS / TOTAL_PROT
    g_log, w = [], []

    def first_column(h):
        g_log.append(col_wait(0, h, log_sum))
        w.append(jnp.exp2(peak[h] - g_log[h]))
        return w[h] * ratio

    row_step(1, first_column)
    for a, r in enumerate(blocks):
        peaks[r, :] = to_tile(w[a // 4][a % 4 : a % 4 + 1, :])
    spread(0, 1.0 / row_wait(1, 0, total))
    for r in blocks:
        part[r, :] = col_terms(r, groups[0])
    spread(1, 1.0 / row_wait(1, 1, total))
    for h in (0, 1):
        rows = [to_row(part[r, :] + col_terms(r, groups[1]), jnp.sum) for r in blocks[4 * h : 4 * h + 4]]
        col_send(1, h, [w[h][a : a + 1, :] * row for a, row in enumerate(rows)])
    row_step(2, lambda h: w[h] * ratio / col_wait(1, h, total))
    w, g_log = jnp.concatenate(w, axis=0), jnp.concatenate(g_log, axis=0)

    def scale_rows(h):
        for a in range(8 * h, 8 * h + 8):
            r = slice(128 * a, 128 * (a + 1))
            t, l = split(e_ref[r, :] * twice(to_tile(rb_ref[:, r])))
            eh2[r, :] = t
            el2[r, :] = l

    def product(r, k):
        h = hi_ref[r, k]
        return nn(h, eh2[k, :]) + nn(h, el2[k, :]) + nn(lo_ref[r, k], eh2[k, :])

    spread(0, 1.0 / row_wait(2, 0, total))
    scale_rows(0)
    first = slice(PARTS[0][0], PARTS[0][0] + PARTS[0][1])
    sums[first, :] = product(first, half(0))
    spread(1, 1.0 / row_wait(2, 1, total))
    scale_rows(1)

    def rows_of(base, unit, index):
        return pl.ds(pl.multiple_of(base + unit * index, 8), unit)

    n_x, n_y = (NX, x, x_peers, lambda d: xy_dev(d, 0)), (NY, y, y_peers, lambda d: xy_dev(0, d))

    def plan(p):
        base, size, first = PARTS[p]
        one, two = (n_x, n_y) if first == "x" else (n_y, n_x)
        return base, size, one, two, size // one[0], size // NDP

    def scatter_one(p):
        base, size, (n, me, peers, dev), _, c1, _ = plan(p)
        for d in peers:
            send(sums.at[rows_of(base, c1, lax.rem(me + d, n))], b1s[p].at[me], fs.at[4 * p], fr.at[4 * p], dev(d))
        b1s[p][me] = sums[rows_of(base, c1, me), :]

    def scatter_two(p):
        _, size, (n1, _, _, _), (n, me, peers, dev), c1, c2 = plan(p)
        await_bytes(b1s[p].at[pl.ds(0, n1 - 1)], fr.at[4 * p])
        mids[p][...] = total([b1s[p][d] for d in range(n1)])
        for d in peers:
            send(mids[p].at[rows_of(0, c2, lax.rem(me + d, n))], b2s[p].at[me], fs.at[4 * p + 1], fr.at[4 * p + 1], dev(d))
        b2s[p][me] = mids[p][rows_of(0, c2, me), :]

    def gather_one(p):
        base, size, (_, me1, _, _), (n, me, peers, dev), c1, c2 = plan(p)
        await_bytes(b2s[p].at[pl.ds(0, n - 1)], fr.at[4 * p + 1])
        own = rows_of(base, c2, me1 * n + me)
        v = total([b2s[p][d] for d in range(n)]) * twice(part[own, :])
        out[own, :] = v * lax.rsqrt(jnp.mean(v * v, axis=1, keepdims=True) + 1e-06)
        for d in peers:
            arrived = fr.at[4 * p + 2] if PARTS[p][2] == "y" else gr.at[NY * p + d]
            send(out.at[own], out.at[own], fs.at[4 * p + 2], arrived, dev(d))
        if PARTS[p][2] == "x":
            for d in x_peers:
                send(out.at[own], out.at[own], fs.at[4 * p + 3], fr.at[4 * p + 3], xy_dev(d, 0))

    def gather_two(p):
        base, size, (_, me, peers, dev), _, c1, c2 = plan(p)
        if PARTS[p][2] == "y":
            await_bytes(out.at[pl.ds(0, c1 - c2)], fr.at[4 * p + 2])
            mid = rows_of(base, c1, me)
            for d in peers:
                send(out.at[mid], out.at[mid], fs.at[4 * p + 3], fr.at[4 * p + 3], dev(d))
            return
        for e in (1, 7, 2, 6, 3, 5, 4):
            got = rows_of(base + c1 * x, c2, lax.rem(y + NY - e, NY))
            await_bytes(out.at[got], gr.at[NY * p + e])
            for d in x_peers:
                send(out.at[got], out.at[got], fs.at[4 * p + 3], fr.at[4 * p + 3], xy_dev(d, 0))

    for p, (base, size, _) in enumerate(PARTS):
        rows = slice(base, base + size)
        acc = sums[rows, :] + product(rows, half(1)) if p == 0 else product(rows, slice(0, ROWS))
        sums[rows, :] = acc * twice(peaks[rows, :])
        scatter_one(p)
        if p == 1:
            c3x[x] = w * jnp.concatenate([to_row(col_terms(r, range(NCH)), jnp.sum) for r in blocks], axis=0)
            for d in x_peers:
                send(c3x.at[x], c3x.at[x], cs.at[4], cr.at[4], xy_dev(d, 0))

    scatter_two(1)
    await_bytes(c3x.at[pl.ds(0, NX - 1)], cr.at[4])
    c3y[y] = total([c3x[d] for d in range(NX)])
    for d in y_peers:
        send(c3y.at[y], c3y.at[y], cs.at[5], cr.at[5], xy_dev(0, d))
    scatter_two(2)
    scatter_two(0)
    scatter_two(3)
    await_bytes(c3y.at[pl.ds(0, NY - 1)], cr.at[5])
    mass = total([c3y[d] for d in range(NY)])
    pot_ref[...] = ((math.log(TOTAL_ROWS / TOTAL_PROT) - LN2 * g_log) - jnp.log(mass)).reshape(pot_ref.shape)
    for a, r in enumerate(blocks):
        part[r, :] = to_tile(1.0 / mass[a : a + 1, :])
    for p in (1, 0, 2, 3):
        gather_one(p)
    for p in (1, 0, 2, 3):
        gather_two(p)
    for p in (0, 1, 2, 3):
        _, size, _, _, c1, c2 = plan(p)
        await_bytes(out.at[pl.ds(0, size - c1)], fr.at[4 * p + 3])
        for n, sent in enumerate((size - c1, c1 - c2, c1 - c2, size - c1)):
            await_bytes(sums.at[pl.ds(0, sent)], fs.at[4 * p + n])

    for n in range(4):
        await_bytes(xy_buf.at[n // 2, n % 2, pl.ds(0, NDP - 1)], cs.at[n])
    for n in range(6):
        await_bytes(z_buf.at[n // 2, n % 2, pl.ds(0, NB - 1)], zs.at[n])
    await_bytes(c3x.at[pl.ds(0, NX - 1)], cs.at[4])
    await_bytes(c3y.at[pl.ds(0, NY - 1)], cs.at[5])


def body(embeddings, prototypes):
    vm = pltpu.VMEM
    dma = pltpu.SemaphoreType.DMA
    counts = [(NX, NY) if first == "x" else (NY, NX) for _, _, first in PARTS]
    sizes = [size for _, size, _ in PARTS]
    new_protos, pot = pl.pallas_call(
        kernel,
        out_shape=(pltpu.VMEM((PROT, DW), F32), pltpu.VMEM((PROT,), F32)),
        in_specs=[pl.BlockSpec(memory_space=pl.ANY)] * 2,
        out_specs=(pl.BlockSpec(memory_space=vm), pl.BlockSpec(memory_space=vm)),
        scratch_shapes=[
            vm((ROWS, DW), F32),
            vm((PROT, DW), F32),
            vm((PROT, 3 * DW), BF16),
            *[vm((PROT, CH), F32) for _ in range(NCH)],
            *[vm((a, s // a, DW), F32) for (a, _), s in zip(counts, sizes)],
            *[vm((s // a, DW), F32) for (a, _), s in zip(counts, sizes)],
            *[vm((b, s // NDP, DW), F32) for (_, b), s in zip(counts, sizes)],
            vm((PROT, ROWS), BF16),
            vm((PROT, ROWS), BF16),
            vm((PROT, 128), F32),
            vm((PROT, 128), F32),
            vm((PROT, 128), F32),
            vm((ROWS, DW), BF16),
            vm((ROWS, DW), BF16),
            vm((1, ROWS), F32),
            vm((3, 2, NB, 8, 128), F32),
            vm((2, 2, NDP, 4, 128), F32),
            vm((NX, 8, 128), F32),
            vm((NY, 8, 128), F32),
            vm((PROT, DW), F32),
            dma((NCH + PROT // CH,)),
            dma((6,)), dma((6,)),
            dma((6,)), dma((6,)),
            dma((4 * len(PARTS),)), dma((4 * len(PARTS),)), dma((NY * len(PARTS),)),
        ],
        compiler_params=pltpu.CompilerParams(
            collective_id=0, has_side_effects=True, vmem_limit_bytes=56 * 1024 * 1024),
        name="sinkhorn",
    )(embeddings, prototypes)
    return new_protos, pot


def solution(mesh):
    in_specs = (P("dp", None), P("bucket", None))
    out_specs = (P("bucket", None), P("bucket"))
    return jax.shard_map(body, mesh=mesh, in_specs=in_specs, out_specs=out_specs, check_vma=False)
```
